32 devices in a mesh: groups: 2 (over y), mem: 8 (over z, x), lat: 2 (over core).
Axes of the slice: x: 2, y: 2, z: 4, core: 2. Of those that a mesh axis runs over, the one named last changes fastest.
Arguments:
- ensemble: float32 [16, 6, 256, 512], P(('groups', 'mem'), None, 'lat'), parts along dimension 0, may hold values from -1.5 to 1.5
- forcing_table: float32 [8, 256, 512], P(None, 'lat'), may hold values from -3 to 3
- ancestors: int32 [16], P('groups'), parts along dimension 0, may hold values from 0 to 7
- selector: int32 [16], P(('groups', 'mem')), parts along dimension 0, may hold values from 0 to 7
Outputs:
- advanced: float32 [16, 6, 256, 512], P(('groups', 'mem'), None, 'lat'), parts along dimension 0
The draws below stay inside these ranges and needn't reach their ends.
There are 2 independent parts, one for each index of `groups`. The reference program is written for one: setup_inputs(seed, part) draws one part's arguments, and reference() takes and returns one part's arrays. A program takes and returns all parts, laid end to end along the dimension named above; an argument that names none is the same for every part. Nothing has to cross between parts.
Inputs may be any that keep to these rules, and one draw needn't show every extreme that they name: `ancestors`: index of a member of the same ensemble; some parents are named by several slots, many by none. `selector`: index of a forcing pattern.
All inputs are finite; a program needn't handle non-finite values.
Results may differ from the reference program's by a relative error of at most 0.00002.
Values sent between devices are 32-bit elements; how exact they have to be, the bound alone decides.
A program may use at most 192 MiB of HBM per device.

```python
import math
import jax
import jax.numpy as jnp
import numpy as np

MEMBERS = 8
NLAT = 256
NLON = 512
NFORCE = 8
STEPS = 3


def place_ends(drawn, rng, smallest, largest):
    longest = drawn.shape.index(max(drawn.shape))
    spots = []
    for shift in (0, 1):
        where = [jax.random.randint(jax.random.fold_in(rng, axis), (), 0, length) for axis, length in enumerate(drawn.shape)]
        where[longest] = (where[longest] + shift) % drawn.shape[longest]
        spots.append(tuple(where))
    return drawn.at[spots[0]].set(smallest).at[spots[1]].set(largest)


def block_scale(own_key, dims, split, low, largest):
    def one(axis_at, parts):
        draws = jax.random.uniform(jax.random.fold_in(jax.random.fold_in(own_key, 6), axis_at), (parts,), jnp.float32, low / len(split), largest / len(split))
        return jnp.repeat(jnp.exp(draws), dims[axis_at] // parts).reshape((-1,) + (1,) * (len(dims) - axis_at - 1))

    factor_of = one(*split[0])
    for cut in split[1:]:
        factor_of = factor_of * one(*cut)
    return factor_of


def rank_bounds(count, slope):
    weights = [(1 << 20) // math.isqrt(rank ** slope) + 1 for rank in range(1, count + 1)]
    width = 1 + sum(weights) // (1 << 30)
    return np.cumsum(np.array([max(1, weight // width) for weight in weights]))


def ranked_ids(rng, dims, count, skew):
    table = rank_bounds(count, skew)
    lot = jax.random.randint(jax.random.fold_in(rng, 1), dims, 0, int(table[count - 1]))
    rank = jnp.searchsorted(jnp.asarray(table, jnp.int32), lot, side="right")
    return jax.random.permutation(jax.random.fold_in(rng, 2), count)[rank].astype(jnp.int32)


def normal_values(own_key, shape, deviation, most, shards=(), kind=jnp.bfloat16):
    result = jax.random.normal(own_key, shape, jnp.float32) * deviation
    if len(shards) > 0:
        result = block_scale(own_key, shape, shards, -0.22, 0.18) * result
    return jnp.clip(result, min=-most, max=most).astype(kind)


def setup_inputs(seed: int = 0, part: int = 0) -> dict:
    arg_keys = jax.random.split(jax.random.key(seed), 5)
    part_splits = jax.random.split(jax.random.fold_in(arg_keys[4], part), 5)
    return {
        "ensemble": normal_values(part_splits[0], (MEMBERS, 6, NLAT, NLON), 0.3, 1.5, ((0, 8), (2, 2)), jnp.float32),
        "forcing_table": normal_values(arg_keys[1], (NFORCE, NLAT, NLON), 0.5, 3.0, ((1, 2),), jnp.float32),
        "ancestors": place_ends(ranked_ids(part_splits[2], (MEMBERS,), MEMBERS, 2), jax.random.fold_in(part_splits[2], 3), 0, MEMBERS - 1).astype(jnp.int32),
        "selector": place_ends(jax.random.randint(part_splits[3], (MEMBERS,), 0, NFORCE), jax.random.fold_in(part_splits[3], 1), 0, NFORCE - 1).astype(jnp.int32),
    }


TIME_STEP = 0.25
DENSITY_RATIO = 0.9
DRAG_RATE = 0.1
CORIOLIS_MEAN = 0.5


def row_below(values):
    widths = [(0, 0)] * (values.ndim - 2) + [(1, 0), (0, 0)]
    return jnp.pad(values[..., :-1, :], widths)


def row_above(values):
    widths = [(0, 0)] * (values.ndim - 2) + [(0, 1), (0, 0)]
    return jnp.pad(values[..., 1:, :], widths)


def col_west(values):
    return jnp.roll(values, 1, axis=-1)


def col_east(values):
    return jnp.roll(values, -1, axis=-1)


def advance(fields, forcing, row_ids, total):
    inside = ((row_ids >= 0.0) & (row_ids < total)).astype(jnp.float32)[:, None]
    wall_mask = ((row_ids >= 1.0) & (row_ids < total)).astype(jnp.float32)[:, None]
    coriolis_u = CORIOLIS_MEAN + (row_ids / total - 0.5)[:, None]
    coriolis_v = CORIOLIS_MEAN + ((row_ids - 0.5) / total - 0.5)[:, None]
    heights = []
    zonal = []
    merid = []
    for layer_index in range(2):
        height = fields[:, 3 * layer_index]
        speed_u = fields[:, 3 * layer_index + 1]
        speed_v = fields[:, 3 * layer_index + 2] * wall_mask
        thickness = 1.0 + height
        flux_x = speed_u * (0.5 * (thickness + col_west(thickness)))
        flux_y = speed_v * (0.5 * (thickness + row_below(thickness)))
        divergence = (col_east(flux_x) - flux_x) + (row_above(flux_y) - flux_y)
        heights.append(height - TIME_STEP * divergence)
        zonal.append(speed_u)
        merid.append(speed_v)
    pressures = [heights[0] + heights[1], DENSITY_RATIO * heights[0] + heights[1]]
    outputs = []
    for layer_index in range(2):
        speed_u = zonal[layer_index]
        speed_v = merid[layer_index]
        pressure = pressures[layer_index]
        extra = forcing if layer_index == 0 else -DRAG_RATE * speed_u
        above_v = row_above(speed_v)
        mean_v = 0.25 * (speed_v + col_west(speed_v) + above_v + col_west(above_v))
        new_u = speed_u + TIME_STEP * (coriolis_u * mean_v - (pressure - col_west(pressure)) + extra)
        below_u = row_below(speed_u)
        mean_u = 0.25 * (speed_u + col_east(speed_u) + below_u + col_east(below_u))
        new_v = (speed_v + TIME_STEP * (-coriolis_v * mean_u - (pressure - row_below(pressure)))) * wall_mask
        outputs.extend([heights[layer_index] * inside, new_u * inside, new_v * inside])
    return jnp.stack(outputs, axis=1)


def reference(ensemble, forcing_table, ancestors, selector):
    parents = jnp.take(ensemble, ancestors, axis=0)
    patterns = jnp.arange(NFORCE, dtype=jnp.int32)
    chosen = selector[:, None, None, None] == patterns[None, :, None, None]
    slot_forcing = jnp.sum(jnp.where(chosen, forcing_table[None], jnp.float32(0.0)), axis=1)
    row_ids = jnp.arange(NLAT).astype(jnp.float32)
    total = jnp.float32(NLAT)
    fields = parents
    for step_index in range(STEPS):
        fields = advance(fields, slot_forcing, row_ids, total)
    return fields
```

```python
import functools

import jax
import jax.numpy as jnp
from jax import lax
from jax.experimental import pallas as pl
from jax.experimental.pallas import tpu as pltpu
from jax.sharding import PartitionSpec as P

STEPS = 3
TIME_STEP = 0.25
DENSITY_RATIO = 0.9
DRAG_RATE = 0.1
CORIOLIS_MEAN = 0.5
HALO = 8
CHUNK = 8


def col_west(values):
    return pltpu.roll(values, 1, axis=1)


def col_east(values):
    return pltpu.roll(values, values.shape[1] - 1, axis=1)


def window_kernel(lat_count, selector, parents, low, high, table, out, state, other, forcing, sems):
    band_rows, columns = parents.shape[1:]
    first = 2 * HALO
    end = first + band_rows
    copies = [
        (parents, state.at[:, pl.ds(first, band_rows)]),
        (low.at[pl.ds(0, 6)], state.at[:, pl.ds(HALO, HALO)]),
        (high.at[pl.ds(0, 6)], state.at[:, pl.ds(end, HALO)]),
        (table.at[selector[0]], forcing.at[pl.ds(first, band_rows)]),
        (low.at[6], forcing.at[pl.ds(HALO, HALO)]),
        (high.at[6], forcing.at[pl.ds(end, HALO)]),
    ]
    copies = [pltpu.make_async_copy(src, dst, sems.at[i]) for i, (src, dst) in enumerate(copies)]
    for copy in copies:
        copy.start()
    for copy in copies:
        copy.wait()

    lat = lax.axis_index("lat")
    base_row = lat * band_rows
    total = band_rows * lat_count
    tile_rows = lax.broadcasted_iota(jnp.int32, (CHUNK, 128), 0)

    def spread(values):
        return jnp.concatenate([values] * (columns // 128), axis=1)

    wide_rows = lax.broadcasted_iota(jnp.int32, (CHUNK, columns), 0)
    is_first, is_last = wide_rows == 0, wide_rows == CHUNK - 1

    for field in (2, 5):
        walled = spread((base_row + tile_rows >= 1).astype(jnp.float32))
        state[field, first : first + CHUNK, :] *= walled

    def advance(src, dst, start):
        def at(ref, field, shift=0):
            return ref[field, pl.ds(pl.multiple_of(start + shift, CHUNK), CHUNK), :]

        def below(here, ref, field):
            return pltpu.roll(jnp.where(is_last, at(ref, field, -CHUNK), here), 1, axis=0)

        def above(here, ref, field):
            return pltpu.roll(jnp.where(is_first, at(ref, field, CHUNK), here), CHUNK - 1, axis=0)

        rows_int = base_row + (start - first) + tile_rows
        rows = rows_int.astype(jnp.float32)
        wall = spread(((rows_int >= 1) & (rows_int < total)).astype(jnp.float32))
        coriolis_u = spread(CORIOLIS_MEAN + (rows / total - 0.5))
        coriolis_v = spread(CORIOLIS_MEAN + ((rows - 0.5) / total - 0.5))
        layers = []
        for field in (0, 3):
            height, speed_u, speed_v = at(src, field), at(src, field + 1), at(src, field + 2)
            above_v = above(speed_v, src, field + 2)
            thickness = 1.0 + height
            flux_x = speed_u * (0.5 * (thickness + col_west(thickness)))
            flux_y = speed_v * (0.5 * (thickness + (1.0 + below(height, src, field))))
            flux_y_above = above_v * (0.5 * ((1.0 + above(height, src, field)) + thickness))
            divergence = (col_east(flux_x) - flux_x) + (flux_y_above - flux_y)
            new_height = height - TIME_STEP * divergence
            dst[field, pl.ds(start, CHUNK), :] = new_height
            layers.append((new_height, speed_u, speed_v, above_v))
        upper, lower = layers[0][0], layers[1][0]
        upper_below, lower_below = below(upper, dst, 0), below(lower, dst, 3)
        pressures = [upper + lower, DENSITY_RATIO * upper + lower]
        pressures_below = [upper_below + lower_below, DENSITY_RATIO * upper_below + lower_below]
        for layer, field in enumerate((0, 3)):
            _, speed_u, speed_v, above_v = layers[layer]
            pressure = pressures[layer]
            if layer == 0:
                extra = forcing[pl.ds(start, CHUNK), :]
            else:
                extra = -DRAG_RATE * speed_u
            sum_v = speed_v + above_v
            mean_v = 0.25 * (sum_v + col_west(sum_v))
            new_u = speed_u + TIME_STEP * (
                coriolis_u * mean_v - (pressure - col_west(pressure)) + extra
            )
            sum_u = speed_u + below(speed_u, src, field + 1)
            mean_u = 0.25 * (sum_u + col_east(sum_u))
            new_v = speed_v + TIME_STEP * (
                -coriolis_v * mean_u - (pressure - pressures_below[layer])
            )
            dst[field + 1, pl.ds(start, CHUNK), :] = new_u
            dst[field + 2, pl.ds(start, CHUNK), :] = new_v * wall

    src, dst = state, other
    for step in range(STEPS):
        def body(index, carry, src=src, dst=dst):
            advance(src, dst, pl.multiple_of(HALO + index * CHUNK, CHUNK))
            return carry

        lax.fori_loop(0, (band_rows + 2 * HALO) // CHUNK, body, 0)
        src, dst = dst, src
    done = pltpu.make_async_copy(src.at[:, pl.ds(first, band_rows)], out, sems.at[0])
    done.start()
    done.wait()


def run_window(parents, low, high, table, selector, lat_count):
    fields_count, band_rows, columns = parents.shape
    held = (fields_count, band_rows + 4 * HALO, columns)
    return pl.pallas_call(
        functools.partial(window_kernel, lat_count),
        out_shape=jax.ShapeDtypeStruct(parents.shape, jnp.float32),
        in_specs=[pl.BlockSpec(memory_space=pltpu.SMEM)] + [pl.BlockSpec(memory_space=pl.ANY)] * 4,
        out_specs=pl.BlockSpec(memory_space=pl.ANY),
        scratch_shapes=[
            pltpu.VMEM(held, jnp.float32),
            pltpu.VMEM(held, jnp.float32),
            pltpu.VMEM(held[1:], jnp.float32),
            pltpu.SemaphoreType.DMA((6,)),
        ],
        compiler_params=pltpu.CompilerParams(vmem_limit_bytes=24 * 1024 * 1024),
        name="window",
    )(selector, parents, low, high, table)


def copy_members(block, ancestors):
    pieces = lax.all_to_all(block, "mem", split_axis=2, concat_axis=0, tiled=True)
    taken = jnp.take(pieces, ancestors, axis=0)
    return lax.all_to_all(taken, "mem", split_axis=0, concat_axis=2, tiled=True)[0]


def edge_rows(values):
    count = lax.axis_size("lat")
    forward = [(i, i + 1) for i in range(count - 1)]
    backward = [(target, source) for source, target in forward]
    low = lax.ppermute(values[:, -HALO:], "lat", forward)
    high = lax.ppermute(values[:, :HALO], "lat", backward)
    return low, high


def on_device(ensemble, forcing_table, ancestors, selector):
    parents = copy_members(ensemble, ancestors)
    table_edges = jnp.concatenate([forcing_table[:, :HALO], forcing_table[:, -HALO:]], axis=1)
    chosen = lax.dynamic_index_in_dim(table_edges, selector[0], 0)
    ends = jnp.concatenate([parents[:, :HALO], parents[:, -HALO:]], axis=1)
    low, high = edge_rows(jnp.concatenate([ends, chosen], axis=0))
    return run_window(parents, low, high, forcing_table, selector, lax.axis_size("lat"))[None]


def solution(mesh):
    placed = (
        P(("groups", "mem"), None, "lat", None),
        P(None, "lat", None),
        P("groups"),
        P(("groups", "mem")),
    )
    return jax.shard_map(
        on_device,
        mesh=mesh,
        in_specs=placed,
        out_specs=P(("groups", "mem"), None, "lat", None),
        check_vma=False,
    )
```

```python
import functools

import jax
import jax.numpy as jnp
from jax import lax
from jax.experimental import pallas as pl
from jax.experimental.pallas import tpu as pltpu
from jax.sharding import PartitionSpec as P

STEPS = 3
TIME_STEP = 0.25
DENSITY_RATIO = 0.9
DRAG_RATE = 0.1
CORIOLIS_MEAN = 0.5
HALO = 8
CHUNK = 8


def col_west(values):
    return pltpu.roll(values, 1, axis=1)


def col_east(values):
    return pltpu.roll(values, values.shape[1] - 1, axis=1)


def window_kernel(lat_count, selector, parents, low, high, table, out, state, other, forcing, sems):
    band_rows, columns = parents.shape[1:]
    first = 2 * HALO
    end = first + band_rows
    copies = [
        (parents, state.at[:, pl.ds(first, band_rows)]),
        (low.at[pl.ds(0, 6)], state.at[:, pl.ds(HALO, HALO)]),
        (high.at[pl.ds(0, 6)], state.at[:, pl.ds(end, HALO)]),
        (table.at[selector[0]], forcing.at[pl.ds(first, band_rows)]),
        (low.at[6], forcing.at[pl.ds(HALO, HALO)]),
        (high.at[6], forcing.at[pl.ds(end, HALO)]),
    ]
    copies = [pltpu.make_async_copy(src, dst, sems.at[i]) for i, (src, dst) in enumerate(copies)]
    for copy in copies:
        copy.start()
    for copy in copies:
        copy.wait()

    lat = lax.axis_index("lat")
    base_row = lat * band_rows
    total = band_rows * lat_count
    tile_rows = lax.broadcasted_iota(jnp.int32, (CHUNK, 128), 0)

    def spread(values):
        return jnp.concatenate([values] * (columns // 128), axis=1)

    wide_rows = lax.broadcasted_iota(jnp.int32, (CHUNK, columns), 0)
    is_first, is_last = wide_rows == 0, wide_rows == CHUNK - 1

    for field in (2, 5):
        walled = spread((base_row + tile_rows >= 1).astype(jnp.float32))
        state[field, first : first + CHUNK, :] *= walled

    def advance(src, dst, start):
        def at(ref, field, shift=0):
            return ref[field, pl.ds(pl.multiple_of(start + shift, CHUNK), CHUNK), :]

        def below(here, ref, field):
            return pltpu.roll(jnp.where(is_last, at(ref, field, -CHUNK), here), 1, axis=0)

        def above(here, ref, field):
            return pltpu.roll(jnp.where(is_first, at(ref, field, CHUNK), here), CHUNK - 1, axis=0)

        rows_int = base_row + (start - first) + tile_rows
        rows = rows_int.astype(jnp.float32)
        wall = spread(((rows_int >= 1) & (rows_int < total)).astype(jnp.float32))
        coriolis_u = spread(CORIOLIS_MEAN + (rows / total - 0.5))
        coriolis_v = spread(CORIOLIS_MEAN + ((rows - 0.5) / total - 0.5))
        layers = []
        for field in (0, 3):
            height, speed_u, speed_v = at(src, field), at(src, field + 1), at(src, field + 2)
            above_v = above(speed_v, src, field + 2)
            thickness = 1.0 + height
            flux_x = speed_u * (0.5 * (thickness + col_west(thickness)))
            flux_y = speed_v * (0.5 * (thickness + (1.0 + below(height, src, field))))
            flux_y_above = above_v * (0.5 * ((1.0 + above(height, src, field)) + thickness))
            divergence = (col_east(flux_x) - flux_x) + (flux_y_above - flux_y)
            new_height = height - TIME_STEP * divergence
            dst[field, pl.ds(start, CHUNK), :] = new_height
            layers.append((new_height, speed_u, speed_v, above_v))
        upper, lower = layers[0][0], layers[1][0]
        upper_below, lower_below = below(upper, dst, 0), below(lower, dst, 3)
        pressures = [upper + lower, DENSITY_RATIO * upper + lower]
        pressures_below = [upper_below + lower_below, DENSITY_RATIO * upper_below + lower_below]
        for layer, field in enumerate((0, 3)):
            _, speed_u, speed_v, above_v = layers[layer]
            pressure = pressures[layer]
            if layer == 0:
                extra = forcing[pl.ds(start, CHUNK), :]
            else:
                extra = -DRAG_RATE * speed_u
            sum_v = speed_v + above_v
            mean_v = 0.25 * (sum_v + col_west(sum_v))
            new_u = speed_u + TIME_STEP * (
                coriolis_u * mean_v - (pressure - col_west(pressure)) + extra
            )
            sum_u = speed_u + below(speed_u, src, field + 1)
            mean_u = 0.25 * (sum_u + col_east(sum_u))
            new_v = speed_v + TIME_STEP * (
                -coriolis_v * mean_u - (pressure - pressures_below[layer])
            )
            dst[field + 1, pl.ds(start, CHUNK), :] = new_u
            dst[field + 2, pl.ds(start, CHUNK), :] = new_v * wall

    src, dst = state, other
    for step in range(STEPS):
        def body(index, carry, src=src, dst=dst):
            advance(src, dst, pl.multiple_of(HALO + index * CHUNK, CHUNK))
            return carry

        lax.fori_loop(0, (band_rows + 2 * HALO) // CHUNK, body, 0)
        src, dst = dst, src
    done = pltpu.make_async_copy(src.at[:, pl.ds(first, band_rows)], out, sems.at[0])
    done.start()
    done.wait()


def run_window(parents, low, high, table, selector, lat_count):
    fields_count, band_rows, columns = parents.shape
    held = (fields_count, band_rows + 4 * HALO, columns)
    return pl.pallas_call(
        functools.partial(window_kernel, lat_count),
        out_shape=jax.ShapeDtypeStruct(parents.shape, jnp.float32),
        in_specs=[pl.BlockSpec(memory_space=pltpu.SMEM)] + [pl.BlockSpec(memory_space=pl.ANY)] * 4,
        out_specs=pl.BlockSpec(memory_space=pl.ANY),
        scratch_shapes=[
            pltpu.VMEM(held, jnp.float32),
            pltpu.VMEM(held, jnp.float32),
            pltpu.VMEM(held[1:], jnp.float32),
            pltpu.SemaphoreType.DMA((6,)),
        ],
        compiler_params=pltpu.CompilerParams(vmem_limit_bytes=24 * 1024 * 1024),
        name="window",
    )(selector, parents, low, high, table)

MESH = pl.DeviceIdType.MESH
PAIR = 2
HALF = 2 * PAIR


def gather_kernel(
    crossing, picks, places, block, forced, out, low, high, *scratch
):
    fields_count, band_rows = block.shape[:2]
    near, far = scratch[:fields_count], scratch[fields_count : 2 * fields_count]
    sent_b, sent_c, zeros, a_send, a_recv, b_send, b_recv, c_send, c_recv = scratch[-12:-3]
    e_send, e_recv, local = scratch[-3:]
    part = band_rows // PAIR
    mem, lat = lax.axis_index("mem"), lax.axis_index("lat")
    half, own = mem // HALF, mem % HALF
    side = own % PAIR
    inner_at = (1 - half) * PAIR
    inner = own // PAIR == 1 - half
    across = (3 - mem // PAIR) * PAIR + side

    def rows(which):
        return pl.ds(pl.multiple_of(which * part, HALO), part)

    def remote(src, dst, send, recv, target):
        return pltpu.make_async_remote_copy(
            src_ref=src, dst_ref=dst, send_sem=send, recv_sem=recv,
            device_id=target, device_id_type=MESH,
        )

    def slot(local_index):
        return {"mem": half * HALF + local_index}

    def to_inner(f, to, origin):
        return remote(
            block.at[f, rows(to)], near[f].at[origin],
            a_send.at[f, to], a_recv.at[f, origin], slot(inner_at + to),
        )

    def keep(f):
        return pltpu.make_async_copy(block.at[f, rows(side)], near[f].at[own], a_recv.at[f, own])

    def over(f):
        return remote(
            sent_b.at[f], far[f],
            b_send.at[f], b_recv.at[f], {"mem": across},
        )

    def to_slot(f, to, origin):
        return remote(
            sent_c.at[f, to], out.at[f, rows(origin)],
            c_send.at[f, to], c_recv.at[f, origin], slot(to),
        )

    def stay(f):
        return pltpu.make_async_copy(sent_c.at[f, own], out.at[f, rows(side)], c_recv.at[f, side])

    barrier = pltpu.get_barrier_semaphore()
    for step in range(1, HALF):
        pl.semaphore_signal(
            barrier, inc=1, device_id=slot((own + step) % HALF), device_id_type=MESH
        )
    pl.semaphore_signal(barrier, inc=1, device_id={"mem": across}, device_id_type=MESH)
    pl.semaphore_signal(barrier, inc=1, device_id={"lat": 1 - lat}, device_id_type=MESH)
    pl.semaphore_wait(barrier, HALF + 1)

    def send_all(f):
        for to in range(PAIR):
            @pl.when(inner & (side == to))
            def _():
                keep(f).start()

            @pl.when(jnp.logical_not(inner & (side == to)))
            def _():
                to_inner(f, to, own).start()

    for f in range(fields_count):
        send_all(f)

    def forced_edge(at_lat):
        first = HALO if at_lat == 0 else 0
        dst = low if at_lat == 0 else high
        return remote(
            forced.at[:, pl.ds(first, HALO)], dst.at[pl.ds(fields_count, 1)],
            e_send.at[0], e_recv.at[0], {"lat": 1 - lat},
        )

    def fields_edge(at_lat):
        first = band_rows - HALO if at_lat == 0 else 0
        dst = low if at_lat == 0 else high
        return remote(
            out.at[:, pl.ds(first, HALO)], dst.at[pl.ds(0, fields_count)],
            e_send.at[1], e_recv.at[1], {"lat": 1 - lat},
        )

    def blank(at_lat):
        return pltpu.make_async_copy(zeros, low if at_lat == 0 else high, local.at[0])

    zeros[...] = jnp.zeros_like(zeros)
    for at_lat in range(2):
        @pl.when(lat == at_lat)
        def _():
            forced_edge(at_lat).start()
            blank(at_lat).start()

    def pass_over(f):
        for origin in range(HALF):
            @pl.when(own == origin)
            def _():
                keep(f).wait()

            @pl.when(own != origin)
            def _():
                to_inner(f, 0, origin).wait_recv()
        for j in range(crossing):
            sent_b[f, j] = near[f][picks[j]]
        over(f).start()

    def hand_out(f):
        over(f).wait_recv()
        for to in range(HALF):
            place = places[to]
            from_near = near[f][jnp.minimum(place, HALF - 1)]
            from_far = far[f][jnp.maximum(place - HALF, 0)]
            sent_c[f, to] = jnp.where(place < HALF, from_near, from_far)

            @pl.when(own == to)
            def _():
                stay(f).start()

            @pl.when(own != to)
            def _():
                to_slot(f, to, side).start()

    @pl.when(inner)
    def _():
        pass_over(0)
        for f in range(1, fields_count):
            pass_over(f)
            hand_out(f - 1)
        hand_out(fields_count - 1)

    def finish(f):
        for origin in range(PAIR):
            @pl.when(inner & (side == origin))
            def _():
                stay(f).wait()

            @pl.when(jnp.logical_not(inner & (side == origin)))
            def _():
                to_slot(f, 0, origin).wait_recv()

    for f in range(fields_count):
        finish(f)
    for at_lat in range(2):
        @pl.when(lat == at_lat)
        def _():
            fields_edge(at_lat).start()

    def drain(f):
        for to in range(PAIR):
            @pl.when(jnp.logical_not(inner & (side == to)))
            def _():
                to_inner(f, to, own).wait_send()

        @pl.when(inner)
        def _():
            over(f).wait_send()
            for to in range(HALF):
                @pl.when(own != to)
                def _():
                    to_slot(f, to, side).wait_send()

    for f in range(fields_count):
        drain(f)
    for at_lat in range(2):
        @pl.when(lat == at_lat)
        def _():
            blank(at_lat).wait()
            for edge in (forced_edge, fields_edge):
                edge(at_lat).wait_send()
                edge(1 - at_lat).wait_recv()


def gather_parents(crossing, picks, places, block, forced):
    fields_count, band_rows, columns = block.shape
    part = band_rows // PAIR
    edge = jax.ShapeDtypeStruct((fields_count + 1, HALO, columns), jnp.float32)
    return pl.pallas_call(
        functools.partial(gather_kernel, crossing),
        out_shape=[jax.ShapeDtypeStruct(block.shape, jnp.float32), edge, edge],
        in_specs=[pl.BlockSpec(memory_space=pltpu.SMEM)] * 2 + [pl.BlockSpec(memory_space=pl.ANY)] * 2,
        out_specs=[pl.BlockSpec(memory_space=pl.ANY)] * 3,
        scratch_shapes=[
            *[pltpu.VMEM((HALF, part, columns), jnp.float32)] * fields_count,
            *[pltpu.VMEM((crossing, part, columns), jnp.float32)] * fields_count,
            pltpu.VMEM((fields_count, crossing, part, columns), jnp.float32),
            pltpu.VMEM((fields_count, HALF, part, columns), jnp.float32),
            pltpu.VMEM((fields_count + 1, HALO, columns), jnp.float32),
            pltpu.SemaphoreType.DMA((fields_count, PAIR)),
            pltpu.SemaphoreType.DMA((fields_count, HALF)),
            pltpu.SemaphoreType.DMA((fields_count,)),
            pltpu.SemaphoreType.DMA((fields_count,)),
            pltpu.SemaphoreType.DMA((fields_count, HALF)),
            pltpu.SemaphoreType.DMA((fields_count, PAIR)),
            pltpu.SemaphoreType.DMA((2,)),
            pltpu.SemaphoreType.DMA((2,)),
            pltpu.SemaphoreType.DMA((1,)),
        ],
        compiler_params=pltpu.CompilerParams(
            collective_id=crossing, has_side_effects=True, vmem_limit_bytes=24 * 1024 * 1024
        ),
        name="gather_parents",
    )(picks, places, block, forced)


def gather_by_halves(block, forced, ancestors):
    half = lax.axis_index("mem") // HALF
    members = jnp.arange(HALF, dtype=jnp.int32)
    by_half = ancestors.reshape(2, HALF)
    other = (1 - jnp.arange(2, dtype=jnp.int32))[:, None] * HALF + members
    named = jnp.any(by_half[:, :, None] == other[:, None, :], axis=1)
    rank = jnp.sum(named[:, None, :] & (members[None, :] < members[:, None])[None], axis=2)
    counts = jnp.max(jnp.sum(named.astype(jnp.int32), axis=1))
    most = counts
    groups = lax.axis_size("groups")
    for step in range(1, groups):
        moved = lax.ppermute(counts, "groups", [(i, (i + step) % groups) for i in range(groups)])
        most = jnp.maximum(most, moved)
    going = lax.dynamic_index_in_dim(named, 1 - half, 0, keepdims=False)
    going_rank = lax.dynamic_index_in_dim(rank, 1 - half, 0, keepdims=False)
    coming_rank = lax.dynamic_index_in_dim(rank, half, 0, keepdims=False)
    picks = jnp.sum(
        jnp.where(going[None] & (going_rank[None] == members[:, None]), members[None], 0), axis=1
    ).astype(jnp.int32)
    parent = lax.dynamic_index_in_dim(by_half, half, 0, keepdims=False)
    arrived = HALF + jnp.sum(jnp.where(parent[:, None] % HALF == members, coming_rank, 0), axis=1)
    places = jnp.where(parent // HALF == half, parent % HALF, arrived).astype(jnp.int32)
    few = HALF // 2

    def run(crossing):
        return lambda: gather_parents(crossing, picks, places, block, forced)

    return lax.cond(most <= few, run(few), run(HALF))


def copy_members(block, ancestors):
    pieces = lax.all_to_all(block, "mem", split_axis=2, concat_axis=0, tiled=True)
    taken = jnp.take(pieces, ancestors, axis=0)
    return lax.all_to_all(taken, "mem", split_axis=0, concat_axis=2, tiled=True)[0]


def edge_rows(values):
    count = lax.axis_size("lat")
    forward = [(i, i + 1) for i in range(count - 1)]
    backward = [(target, source) for source, target in forward]
    low = lax.ppermute(values[:, -HALO:], "lat", forward)
    high = lax.ppermute(values[:, :HALO], "lat", backward)
    return low, high


def on_device(ensemble, forcing_table, ancestors, selector):
    table_edges = jnp.concatenate([forcing_table[:, :HALO], forcing_table[:, -HALO:]], axis=1)
    chosen = lax.dynamic_index_in_dim(table_edges, selector[0], 0)
    by_halves = lax.axis_size("mem") == 2 * HALF and lax.axis_size("lat") == 2
    if by_halves and ensemble.shape[2] % (PAIR * HALO) == 0:
        parents, low, high = gather_by_halves(ensemble[0], chosen, ancestors)
    else:
        parents = copy_members(ensemble, ancestors)
        ends = jnp.concatenate([parents[:, :HALO], parents[:, -HALO:]], axis=1)
        low, high = edge_rows(jnp.concatenate([ends, chosen], axis=0))
    return run_window(parents, low, high, forcing_table, selector, lax.axis_size("lat"))[None]


def solution(mesh):
    placed = (
        P(("groups", "mem"), None, "lat", None),
        P(None, "lat", None),
        P("groups"),
        P(("groups", "mem")),
    )
    return jax.shard_map(
        on_device,
        mesh=mesh,
        in_specs=placed,
        out_specs=P(("groups", "mem"), None, "lat", None),
        check_vma=False,
    )
```

```python
import functools

import jax
import jax.numpy as jnp
from jax import lax
from jax.experimental import pallas as pl
from jax.experimental.pallas import tpu as pltpu
from jax.sharding import PartitionSpec as P

STEPS = 3
TIME_STEP = 0.25
DENSITY_RATIO = 0.9
DRAG_RATE = 0.1
CORIOLIS_MEAN = 0.5
HALO = 8
MOST_ROWS = 48


def col_west(values):
    return pltpu.roll(values, 1, axis=2)


def col_east(values):
    return pltpu.roll(values, values.shape[2] - 1, axis=2)


def chunk_rows(rows):
    tiles = rows // HALO
    return HALO * max(n for n in range(1, MOST_ROWS // HALO + 1) if tiles % n == 0)


def window_kernel(lat_count, selector, parents, low, high, table, out, state, other, forcing, sems):
    band_rows, columns = parents.shape[1:]
    chunk = chunk_rows(band_rows + 2 * HALO)
    first = 2 * HALO
    end = first + band_rows
    copies = [
        (parents, state.at[:, pl.ds(first, band_rows)]),
        (low.at[pl.ds(0, 6)], state.at[:, pl.ds(HALO, HALO)]),
        (high.at[pl.ds(0, 6)], state.at[:, pl.ds(end, HALO)]),
        (table.at[selector[0]], forcing.at[pl.ds(first, band_rows)]),
        (low.at[6], forcing.at[pl.ds(HALO, HALO)]),
        (high.at[6], forcing.at[pl.ds(end, HALO)]),
    ]
    copies = [pltpu.make_async_copy(src, dst, sems.at[i]) for i, (src, dst) in enumerate(copies)]
    for copy in copies:
        copy.start()
    for copy in copies:
        copy.wait()

    lat = lax.axis_index("lat")
    base_row = lat * band_rows
    total = band_rows * lat_count
    tiles = chunk // HALO
    row_in_chunk = HALO * lax.broadcasted_iota(
        jnp.int32, (tiles, HALO, 128), 0
    ) + lax.broadcasted_iota(jnp.int32, (tiles, HALO, 128), 1)
    wide_rows = lax.broadcasted_iota(jnp.int32, (tiles, HALO, columns), 1)
    is_first, is_last = wide_rows == 0, wide_rows == HALO - 1

    def spread(values):
        return jnp.concatenate([values] * (columns // 128), axis=-1)

    for field in (2, 5):
        walled = spread((base_row + row_in_chunk[0] >= 1).astype(jnp.float32))
        state[field, first : first + HALO, :] *= walled

    def advance(src, dst, start):
        def at(ref, field, shift=0, count=tiles):
            here = pl.ds(pl.multiple_of(start + shift, HALO), count * HALO)
            return ref[field, here, :].reshape(count, HALO, columns)

        def below(here, ref, field):
            lower = jnp.concatenate([at(ref, field, -HALO, 1), here[:-1]], axis=0)
            return pltpu.roll(jnp.where(is_last, lower, here), 1, axis=1)

        def above(here, ref, field):
            higher = jnp.concatenate([here[1:], at(ref, field, chunk, 1)], axis=0)
            return pltpu.roll(jnp.where(is_first, higher, here), HALO - 1, axis=1)

        def put(field, values):
            dst[field, pl.ds(start, chunk), :] = values.reshape(chunk, columns)

        rows_int = base_row + (start - first) + row_in_chunk
        rows = rows_int.astype(jnp.float32)
        wall = spread(((rows_int >= 1) & (rows_int < total)).astype(jnp.float32))
        coriolis_u = spread(CORIOLIS_MEAN + (rows / total - 0.5))
        coriolis_v = spread(CORIOLIS_MEAN + ((rows - 0.5) / total - 0.5))
        layers = []
        for field in (0, 3):
            height, speed_u, speed_v = at(src, field), at(src, field + 1), at(src, field + 2)
            above_v = above(speed_v, src, field + 2)
            thickness = 1.0 + height
            flux_x = speed_u * (0.5 * (thickness + col_west(thickness)))
            flux_y = speed_v * (0.5 * (thickness + (1.0 + below(height, src, field))))
            flux_y_above = above_v * (0.5 * ((1.0 + above(height, src, field)) + thickness))
            divergence = (col_east(flux_x) - flux_x) + (flux_y_above - flux_y)
            new_height = height - TIME_STEP * divergence
            put(field, new_height)
            layers.append((new_height, speed_u, speed_v, above_v))
        upper, lower = layers[0][0], layers[1][0]
        upper_below, lower_below = below(upper, dst, 0), below(lower, dst, 3)
        pressures = [upper + lower, DENSITY_RATIO * upper + lower]
        pressures_below = [upper_below + lower_below, DENSITY_RATIO * upper_below + lower_below]
        for layer, field in enumerate((0, 3)):
            _, speed_u, speed_v, above_v = layers[layer]
            pressure = pressures[layer]
            if layer == 0:
                extra = forcing[pl.ds(start, chunk), :].reshape(tiles, HALO, columns)
            else:
                extra = -DRAG_RATE * speed_u
            sum_v = speed_v + above_v
            mean_v = 0.25 * (sum_v + col_west(sum_v))
            new_u = speed_u + TIME_STEP * (
                coriolis_u * mean_v - (pressure - col_west(pressure)) + extra
            )
            sum_u = speed_u + below(speed_u, src, field + 1)
            mean_u = 0.25 * (sum_u + col_east(sum_u))
            new_v = speed_v + TIME_STEP * (
                -coriolis_v * mean_u - (pressure - pressures_below[layer])
            )
            put(field + 1, new_u)
            put(field + 2, new_v * wall)

    src, dst = state, other
    for step in range(STEPS):
        def body(index, carry, src=src, dst=dst):
            advance(src, dst, pl.multiple_of(HALO + index * chunk, HALO))
            return carry

        lax.fori_loop(0, (band_rows + 2 * HALO) // chunk, body, 0)
        src, dst = dst, src
    done = pltpu.make_async_copy(src.at[:, pl.ds(first, band_rows)], out, sems.at[0])
    done.start()
    done.wait()


def run_window(parents, low, high, table, selector, lat_count):
    fields_count, band_rows, columns = parents.shape
    held = (fields_count, band_rows + 4 * HALO, columns)
    return pl.pallas_call(
        functools.partial(window_kernel, lat_count),
        out_shape=jax.ShapeDtypeStruct(parents.shape, jnp.float32),
        in_specs=[pl.BlockSpec(memory_space=pltpu.SMEM)] + [pl.BlockSpec(memory_space=pl.ANY)] * 4,
        out_specs=pl.BlockSpec(memory_space=pl.ANY),
        scratch_shapes=[
            pltpu.VMEM(held, jnp.float32),
            pltpu.VMEM(held, jnp.float32),
            pltpu.VMEM(held[1:], jnp.float32),
            pltpu.SemaphoreType.DMA((6,)),
        ],
        compiler_params=pltpu.CompilerParams(vmem_limit_bytes=24 * 1024 * 1024),
        name="window",
    )(selector, parents, low, high, table)

MESH = pl.DeviceIdType.MESH
PAIR = 2
HALF = 2 * PAIR


def gather_kernel(
    crossing, ancestors, block, forced, out, low, high, *scratch
):
    fields_count, band_rows = block.shape[:2]
    near, far = scratch[:fields_count], scratch[fields_count : 2 * fields_count]
    sent_b, sent_c, zeros, a_send, a_recv, b_send, b_recv, c_send, c_recv = scratch[-12:-3]
    e_send, e_recv, local = scratch[-3:]
    part = band_rows // PAIR
    mem, lat = lax.axis_index("mem"), lax.axis_index("lat")
    half, own = mem // HALF, mem % HALF
    side = own % PAIR
    inner_at = (1 - half) * PAIR
    inner = own // PAIR == 1 - half
    across = (3 - mem // PAIR) * PAIR + side

    def ranks(wanted, named_half):
        named, rank, before = [], [], jnp.int32(0)
        for m in range(HALF):
            hits = [(one == named_half * HALF + m).astype(jnp.int32) for one in wanted]
            named.append(functools.reduce(jnp.maximum, hits))
            rank.append(before)
            before = before + named[-1]
        return named, rank

    mine = [ancestors[half * HALF + s] for s in range(HALF)]
    theirs = [ancestors[(1 - half) * HALF + s] for s in range(HALF)]
    named, rank = ranks(theirs, half)
    picks = [
        sum(m * named[m] * (rank[m] == j).astype(jnp.int32) for m in range(HALF))
        for j in range(crossing)
    ]
    _, rank = ranks(mine, 1 - half)
    arrived = [
        sum((p == (1 - half) * HALF + m).astype(jnp.int32) * rank[m] for m in range(HALF))
        for p in mine
    ]
    is_near = [p // HALF == half for p in mine]

    def rows(which):
        return pl.ds(pl.multiple_of(which * part, HALO), part)

    def remote(src, dst, send, recv, target):
        return pltpu.make_async_remote_copy(
            src_ref=src, dst_ref=dst, send_sem=send, recv_sem=recv,
            device_id=target, device_id_type=MESH,
        )

    def slot(local_index):
        return {"mem": half * HALF + local_index}

    def to_inner(f, to, origin):
        return remote(
            block.at[f, rows(to)], near[f].at[origin],
            a_send.at[f, to], a_recv.at[f, origin], slot(inner_at + to),
        )

    def keep(f):
        return pltpu.make_async_copy(block.at[f, rows(side)], near[f].at[own], a_recv.at[f, own])

    def over(f):
        return remote(
            sent_b.at[f], far[f],
            b_send.at[f], b_recv.at[f], {"mem": across},
        )

    def to_slot(f, to, origin):
        return remote(
            sent_c.at[f, to], out.at[f, rows(origin)],
            c_send.at[f, to], c_recv.at[f, origin], slot(to),
        )

    def stay(f):
        return pltpu.make_async_copy(sent_c.at[f, own], out.at[f, rows(side)], c_recv.at[f, side])

    barrier = pltpu.get_barrier_semaphore()
    for step in range(1, HALF):
        pl.semaphore_signal(
            barrier, inc=1, device_id=slot((own + step) % HALF), device_id_type=MESH
        )
    pl.semaphore_signal(barrier, inc=1, device_id={"mem": across}, device_id_type=MESH)
    pl.semaphore_signal(barrier, inc=1, device_id={"lat": 1 - lat}, device_id_type=MESH)
    pl.semaphore_wait(barrier, HALF + 1)

    def send_all(f):
        for to in range(PAIR):
            @pl.when(inner & (side == to))
            def _():
                keep(f).start()

            @pl.when(jnp.logical_not(inner & (side == to)))
            def _():
                to_inner(f, to, own).start()

    for f in range(fields_count):
        send_all(f)

    def forced_edge(at_lat):
        first = HALO if at_lat == 0 else 0
        dst = low if at_lat == 0 else high
        return remote(
            forced.at[:, pl.ds(first, HALO)], dst.at[pl.ds(fields_count, 1)],
            e_send.at[0], e_recv.at[0], {"lat": 1 - lat},
        )

    def fields_edge(at_lat):
        first = band_rows - HALO if at_lat == 0 else 0
        dst = low if at_lat == 0 else high
        return remote(
            out.at[:, pl.ds(first, HALO)], dst.at[pl.ds(0, fields_count)],
            e_send.at[1], e_recv.at[1], {"lat": 1 - lat},
        )

    def blank(at_lat):
        return pltpu.make_async_copy(zeros, low if at_lat == 0 else high, local.at[0])

    zeros[...] = jnp.zeros_like(zeros)
    for at_lat in range(2):
        @pl.when(lat == at_lat)
        def _():
            forced_edge(at_lat).start()
            blank(at_lat).start()

    def pass_over(f):
        for origin in range(HALF):
            @pl.when(own == origin)
            def _():
                keep(f).wait()

            @pl.when(own != origin)
            def _():
                to_inner(f, 0, origin).wait_recv()
        for j in range(crossing):
            sent_b[f, j] = near[f][picks[j]]
        over(f).start()

    def hand_out(f):
        over(f).wait_recv()
        for to in range(HALF):
            from_near = near[f][mine[to] % HALF]
            from_far = far[f][arrived[to]]
            sent_c[f, to] = jnp.where(is_near[to], from_near, from_far)

            @pl.when(own == to)
            def _():
                stay(f).start()

            @pl.when(own != to)
            def _():
                to_slot(f, to, side).start()

    @pl.when(inner)
    def _():
        pass_over(0)
        for f in range(1, fields_count):
            pass_over(f)
            hand_out(f - 1)
        hand_out(fields_count - 1)

    def finish(f):
        for origin in range(PAIR):
            @pl.when(inner & (side == origin))
            def _():
                stay(f).wait()

            @pl.when(jnp.logical_not(inner & (side == origin)))
            def _():
                to_slot(f, 0, origin).wait_recv()

    for f in range(fields_count):
        finish(f)
    for at_lat in range(2):
        @pl.when(lat == at_lat)
        def _():
            fields_edge(at_lat).start()

    def drain(f):
        for to in range(PAIR):
            @pl.when(jnp.logical_not(inner & (side == to)))
            def _():
                to_inner(f, to, own).wait_send()

        @pl.when(inner)
        def _():
            over(f).wait_send()
            for to in range(HALF):
                @pl.when(own != to)
                def _():
                    to_slot(f, to, side).wait_send()

    for f in range(fields_count):
        drain(f)
    for at_lat in range(2):
        @pl.when(lat == at_lat)
        def _():
            blank(at_lat).wait()
            for edge in (forced_edge, fields_edge):
                edge(at_lat).wait_send()
                edge(1 - at_lat).wait_recv()


def gather_parents(crossing, ancestors, block, forced):
    fields_count, band_rows, columns = block.shape
    part = band_rows // PAIR
    edge = jax.ShapeDtypeStruct((fields_count + 1, HALO, columns), jnp.float32)
    return pl.pallas_call(
        functools.partial(gather_kernel, crossing),
        out_shape=[jax.ShapeDtypeStruct(block.shape, jnp.float32), edge, edge],
        in_specs=[pl.BlockSpec(memory_space=pltpu.SMEM)] + [pl.BlockSpec(memory_space=pl.ANY)] * 2,
        out_specs=[pl.BlockSpec(memory_space=pl.ANY)] * 3,
        scratch_shapes=[
            *[pltpu.VMEM((HALF, part, columns), jnp.float32)] * fields_count,
            *[pltpu.VMEM((crossing, part, columns), jnp.float32)] * fields_count,
            pltpu.VMEM((fields_count, crossing, part, columns), jnp.float32),
            pltpu.VMEM((fields_count, HALF, part, columns), jnp.float32),
            pltpu.VMEM((fields_count + 1, HALO, columns), jnp.float32),
            pltpu.SemaphoreType.DMA((fields_count, PAIR)),
            pltpu.SemaphoreType.DMA((fields_count, HALF)),
            pltpu.SemaphoreType.DMA((fields_count,)),
            pltpu.SemaphoreType.DMA((fields_count,)),
            pltpu.SemaphoreType.DMA((fields_count, HALF)),
            pltpu.SemaphoreType.DMA((fields_count, PAIR)),
            pltpu.SemaphoreType.DMA((2,)),
            pltpu.SemaphoreType.DMA((2,)),
            pltpu.SemaphoreType.DMA((1,)),
        ],
        compiler_params=pltpu.CompilerParams(
            collective_id=crossing, has_side_effects=True, vmem_limit_bytes=24 * 1024 * 1024
        ),
        name="gather_parents",
    )(ancestors, block, forced)


def gather_by_halves(block, forced, ancestors):
    groups = lax.axis_size("groups")
    lists = [ancestors] + [
        lax.ppermute(ancestors, "groups", [(i, (i + step) % groups) for i in range(groups)])
        for step in range(1, groups)
    ]
    by_half = jnp.stack(lists).reshape(groups, 2, 1, HALF)
    members = jnp.arange(2 * HALF, dtype=jnp.int32).reshape(2, HALF)[::-1, :, None]
    named = jnp.any(by_half == members, axis=-1)
    most = jnp.max(jnp.sum(named.astype(jnp.int32), axis=-1))
    few = HALF // 2

    def run(crossing):
        return lambda: gather_parents(crossing, ancestors, block, forced)

    return lax.cond(most <= few, run(few), run(HALF))


def copy_members(block, ancestors):
    pieces = lax.all_to_all(block, "mem", split_axis=2, concat_axis=0, tiled=True)
    taken = jnp.take(pieces, ancestors, axis=0)
    return lax.all_to_all(taken, "mem", split_axis=0, concat_axis=2, tiled=True)[0]


def edge_rows(values):
    count = lax.axis_size("lat")
    forward = [(i, i + 1) for i in range(count - 1)]
    backward = [(target, source) for source, target in forward]
    low = lax.ppermute(values[:, -HALO:], "lat", forward)
    high = lax.ppermute(values[:, :HALO], "lat", backward)
    return low, high


def on_device(ensemble, forcing_table, ancestors, selector):
    table_edges = jnp.concatenate([forcing_table[:, :HALO], forcing_table[:, -HALO:]], axis=1)
    chosen = lax.dynamic_index_in_dim(table_edges, selector[0], 0)
    by_halves = lax.axis_size("mem") == 2 * HALF and lax.axis_size("lat") == 2
    if by_halves and ensemble.shape[2] % (PAIR * HALO) == 0:
        parents, low, high = gather_by_halves(ensemble[0], chosen, ancestors)
    else:
        parents = copy_members(ensemble, ancestors)
        ends = jnp.concatenate([parents[:, :HALO], parents[:, -HALO:]], axis=1)
        low, high = edge_rows(jnp.concatenate([ends, chosen], axis=0))
    return run_window(parents, low, high, forcing_table, selector, lax.axis_size("lat"))[None]


def solution(mesh):
    placed = (
        P(("groups", "mem"), None, "lat", None),
        P(None, "lat", None),
        P("groups"),
        P(("groups", "mem")),
    )
    return jax.shard_map(
        on_device,
        mesh=mesh,
        in_specs=placed,
        out_specs=P(("groups", "mem"), None, "lat", None),
        check_vma=False,
    )
```

```python
import functools

import jax
import jax.numpy as jnp
from jax import lax
from jax.experimental import pallas as pl
from jax.experimental.pallas import tpu as pltpu
from jax.sharding import PartitionSpec as P

STEPS = 3
TIME_STEP = 0.25
DENSITY_RATIO = 0.9
DRAG_RATE = 0.1
CORIOLIS_MEAN = 0.5
HALO = 8
MOST_ROWS = 48


def col_west(values):
    return pltpu.roll(values, 1, axis=2)


def col_east(values):
    return pltpu.roll(values, values.shape[2] - 1, axis=2)


def chunk_rows(rows):
    tiles = rows // HALO
    return HALO * max(n for n in range(1, MOST_ROWS // HALO + 1) if tiles % n == 0)


def window_kernel(lat_count, selector, parents, low, high, table, out, state, other, forcing, sems):
    band_rows, columns = parents.shape[1:]
    chunk = chunk_rows(band_rows + 2 * HALO)
    first = 2 * HALO
    end = first + band_rows
    copies = [
        (parents, state.at[:, pl.ds(first, band_rows)]),
        (low.at[pl.ds(0, 6)], state.at[:, pl.ds(HALO, HALO)]),
        (high.at[pl.ds(0, 6)], state.at[:, pl.ds(end, HALO)]),
        (table.at[selector[0]], forcing.at[pl.ds(first, band_rows)]),
        (low.at[6], forcing.at[pl.ds(HALO, HALO)]),
        (high.at[6], forcing.at[pl.ds(end, HALO)]),
    ]
    copies = [pltpu.make_async_copy(src, dst, sems.at[i]) for i, (src, dst) in enumerate(copies)]
    for copy in copies:
        copy.start()
    for copy in copies:
        copy.wait()

    lat = lax.axis_index("lat")
    base_row = lat * band_rows
    total = band_rows * lat_count
    tiles = chunk // HALO
    row_in_chunk = HALO * lax.broadcasted_iota(
        jnp.int32, (tiles, HALO, 128), 0
    ) + lax.broadcasted_iota(jnp.int32, (tiles, HALO, 128), 1)
    wide_rows = lax.broadcasted_iota(jnp.int32, (tiles, HALO, columns), 1)
    is_first, is_last = wide_rows == 0, wide_rows == HALO - 1

    def spread(values):
        return jnp.concatenate([values] * (columns // 128), axis=-1)

    for field in (2, 5):
        walled = spread((base_row + row_in_chunk[0] >= 1).astype(jnp.float32))
        state[field, first : first + HALO, :] *= walled

    def advance(src, dst, start):
        def at(ref, field, shift=0, count=tiles):
            here = pl.ds(pl.multiple_of(start + shift, HALO), count * HALO)
            return ref[field, here, :].reshape(count, HALO, columns)

        def below(here, ref, field):
            lower = jnp.concatenate([at(ref, field, -HALO, 1), here[:-1]], axis=0)
            return pltpu.roll(jnp.where(is_last, lower, here), 1, axis=1)

        def above(here, ref, field):
            higher = jnp.concatenate([here[1:], at(ref, field, chunk, 1)], axis=0)
            return pltpu.roll(jnp.where(is_first, higher, here), HALO - 1, axis=1)

        def put(field, values):
            dst[field, pl.ds(start, chunk), :] = values.reshape(chunk, columns)

        rows_int = base_row + (start - first) + row_in_chunk
        rows = rows_int.astype(jnp.float32)
        wall = spread(((rows_int >= 1) & (rows_int < total)).astype(jnp.float32))
        coriolis_u = spread(CORIOLIS_MEAN + (rows / total - 0.5))
        coriolis_v = spread(CORIOLIS_MEAN + ((rows - 0.5) / total - 0.5))
        layers = []
        for field in (0, 3):
            height, speed_u, speed_v = at(src, field), at(src, field + 1), at(src, field + 2)
            above_v = above(speed_v, src, field + 2)
            thickness = 1.0 + height
            flux_x = speed_u * (0.5 * (thickness + col_west(thickness)))
            flux_y = speed_v * (0.5 * (thickness + (1.0 + below(height, src, field))))
            flux_y_above = above_v * (0.5 * ((1.0 + above(height, src, field)) + thickness))
            divergence = (col_east(flux_x) - flux_x) + (flux_y_above - flux_y)
            new_height = height - TIME_STEP * divergence
            put(field, new_height)
            layers.append((new_height, speed_u, speed_v, above_v))
        upper, lower = layers[0][0], layers[1][0]
        upper_below, lower_below = below(upper, dst, 0), below(lower, dst, 3)
        pressures = [upper + lower, DENSITY_RATIO * upper + lower]
        pressures_below = [upper_below + lower_below, DENSITY_RATIO * upper_below + lower_below]
        for layer, field in enumerate((0, 3)):
            _, speed_u, speed_v, above_v = layers[layer]
            pressure = pressures[layer]
            if layer == 0:
                extra = forcing[pl.ds(start, chunk), :].reshape(tiles, HALO, columns)
            else:
                extra = -DRAG_RATE * speed_u
            sum_v = speed_v + above_v
            mean_v = 0.25 * (sum_v + col_west(sum_v))
            new_u = speed_u + TIME_STEP * (
                coriolis_u * mean_v - (pressure - col_west(pressure)) + extra
            )
            sum_u = speed_u + below(speed_u, src, field + 1)
            mean_u = 0.25 * (sum_u + col_east(sum_u))
            new_v = speed_v + TIME_STEP * (
                -coriolis_v * mean_u - (pressure - pressures_below[layer])
            )
            put(field + 1, new_u)
            put(field + 2, new_v * wall)

    src, dst = state, other
    for step in range(STEPS):
        def body(index, carry, src=src, dst=dst):
            advance(src, dst, pl.multiple_of(HALO + index * chunk, HALO))
            return carry

        lax.fori_loop(0, (band_rows + 2 * HALO) // chunk, body, 0)
        src, dst = dst, src
    done = pltpu.make_async_copy(src.at[:, pl.ds(first, band_rows)], out, sems.at[0])
    done.start()
    done.wait()


def run_window(parents, low, high, table, selector, lat_count):
    fields_count, band_rows, columns = parents.shape
    held = (fields_count, band_rows + 4 * HALO, columns)
    return pl.pallas_call(
        functools.partial(window_kernel, lat_count),
        out_shape=jax.ShapeDtypeStruct(parents.shape, jnp.float32),
        in_specs=[pl.BlockSpec(memory_space=pltpu.SMEM)] + [pl.BlockSpec(memory_space=pl.ANY)] * 4,
        out_specs=pl.BlockSpec(memory_space=pl.ANY),
        scratch_shapes=[
            pltpu.VMEM(held, jnp.float32),
            pltpu.VMEM(held, jnp.float32),
            pltpu.VMEM(held[1:], jnp.float32),
            pltpu.SemaphoreType.DMA((6,)),
        ],
        compiler_params=pltpu.CompilerParams(vmem_limit_bytes=24 * 1024 * 1024),
        name="window",
    )(selector, parents, low, high, table)


MESH = pl.DeviceIdType.MESH
PAIR = 2
HALF = 2 * PAIR
CUTS = 2
LAG = 2


def other_half_count(lists_count, *refs):
    lists, out = refs[:lists_count], refs[lists_count]
    most = jnp.int32(0)
    for ancestors in lists:
        for half in range(2):
            wanted = [ancestors[half * HALF + s] for s in range(HALF)]
            most = jnp.maximum(most, ranks(wanted, 1 - half)[2])
    out[0] = most


def ranks(wanted, named_half):
    named, rank, before = [], [], jnp.int32(0)
    for m in range(HALF):
        hits = [(one == named_half * HALF + m).astype(jnp.int32) for one in wanted]
        named.append(functools.reduce(jnp.maximum, hits))
        rank.append(before)
        before = before + named[-1]
    return named, rank, before


def gather_kernel(crossing, ancestors, block, forced, out, low, high, *scratch):
    fields_count, band_rows = block.shape[:2]
    pieces = fields_count * CUTS
    part = band_rows // PAIR
    piece_rows = part // CUTS
    near, far = scratch[:pieces], scratch[pieces : 2 * pieces]
    sent_b, sent_c, relayed, zeros = scratch[2 * pieces : 2 * pieces + 4]
    a_send, a_recv, b_send, b_recv, c_send, c_recv, r_recv = scratch[-10:-3]
    e_send, e_recv, local = scratch[-3:]
    mem, lat = lax.axis_index("mem"), lax.axis_index("lat")
    half, own = mem // HALF, mem % HALF
    side = own % PAIR
    inner_at = (1 - half) * PAIR
    outer_at = half * PAIR
    inner = own // PAIR == 1 - half
    outer = jnp.logical_not(inner)
    across = (3 - mem // PAIR) * PAIR + side

    mine = [ancestors[half * HALF + s] for s in range(HALF)]
    theirs = [ancestors[(1 - half) * HALF + s] for s in range(HALF)]
    named, rank, _ = ranks(theirs, half)
    picks = [
        sum(m * named[m] * (rank[m] == j).astype(jnp.int32) for m in range(HALF))
        for j in range(crossing)
    ]
    _, rank, _ = ranks(mine, 1 - half)
    arrived = [
        sum((p == (1 - half) * HALF + m).astype(jnp.int32) * rank[m] for m in range(HALF))
        for p in mine
    ]
    is_near = [p // HALF == half for p in mine]

    def piece(ref, c, which):
        start = which * part + c % CUTS * piece_rows
        return ref.at[c // CUTS, pl.ds(pl.multiple_of(start, HALO), piece_rows)]

    def remote(src, dst, send, recv, target):
        return pltpu.make_async_remote_copy(
            src_ref=src, dst_ref=dst, send_sem=send, recv_sem=recv,
            device_id=target, device_id_type=MESH,
        )

    def slot(local_index):
        return {"mem": half * HALF + local_index}

    def to_inner(c, to, origin):
        return remote(
            piece(block, c, to), near[c].at[origin],
            a_send.at[c, to], a_recv.at[c, origin], slot(inner_at + to),
        )

    def keep(c):
        return pltpu.make_async_copy(piece(block, c, side), near[c].at[own], a_recv.at[c, own])

    def over(c):
        return remote(sent_b.at[c], far[c], b_send.at[c], b_recv.at[c], {"mem": across})

    def to_relay(c):
        return remote(
            sent_c.at[c, 0], relayed.at[c], c_send.at[c, 0], r_recv.at[c], slot(outer_at + side)
        )

    def relay(c, origin):
        return remote(
            relayed.at[c], piece(out, c, origin),
            c_send.at[c, 0], c_recv.at[c, origin], slot(outer_at + 1 - side),
        )

    def to_outer(c, origin):
        return remote(
            sent_c.at[c, 1], piece(out, c, origin),
            c_send.at[c, 1], c_recv.at[c, origin], slot(outer_at + side),
        )

    def to_other(c, origin):
        return remote(
            sent_c.at[c, 2], piece(out, c, origin),
            c_send.at[c, 2], c_recv.at[c, origin], slot(inner_at + 1 - side),
        )

    def stay(c):
        return pltpu.make_async_copy(sent_c.at[c, 3], piece(out, c, side), c_recv.at[c, side])

    barrier = pltpu.get_barrier_semaphore()
    for step in range(1, HALF):
        pl.semaphore_signal(
            barrier, inc=1, device_id=slot((own + step) % HALF), device_id_type=MESH
        )
    pl.semaphore_signal(barrier, inc=1, device_id={"mem": across}, device_id_type=MESH)
    pl.semaphore_signal(barrier, inc=1, device_id={"lat": 1 - lat}, device_id_type=MESH)
    pl.semaphore_wait(barrier, HALF + 1)

    for c in range(pieces):
        for to in range(PAIR):
            @pl.when(inner & (side == to))
            def _():
                keep(c).start()

            @pl.when(jnp.logical_not(inner & (side == to)))
            def _():
                to_inner(c, to, own).start()

    def forced_edge(at_lat):
        first = HALO if at_lat == 0 else 0
        dst = low if at_lat == 0 else high
        return remote(
            forced.at[:, pl.ds(first, HALO)], dst.at[pl.ds(fields_count, 1)],
            e_send.at[0], e_recv.at[0], {"lat": 1 - lat},
        )

    def fields_edge(at_lat):
        first = band_rows - HALO if at_lat == 0 else 0
        dst = low if at_lat == 0 else high
        return remote(
            out.at[:, pl.ds(first, HALO)], dst.at[pl.ds(0, fields_count)],
            e_send.at[1], e_recv.at[1], {"lat": 1 - lat},
        )

    def blank(at_lat):
        return pltpu.make_async_copy(zeros, low if at_lat == 0 else high, local.at[0])

    zeros[...] = jnp.zeros_like(zeros)
    for at_lat in range(2):
        @pl.when(lat == at_lat)
        def _():
            forced_edge(at_lat).start()
            blank(at_lat).start()

    def pass_over(c):
        for origin in range(HALF):
            @pl.when(own == origin)
            def _():
                keep(c).wait()

            @pl.when(own != origin)
            def _():
                to_inner(c, 0, origin).wait_recv()
        for j in range(crossing):
            sent_b[c, j] = near[c][picks[j]]
        over(c).start()

    def parent_of(c, local_index):
        def pick(values):
            return sum(
                values[s] * (local_index == s).astype(jnp.int32) for s in range(HALF)
            )

        from_near = near[c][pick([p % HALF for p in mine])]
        from_far = far[c][pick(arrived)]
        return jnp.where(pick([n.astype(jnp.int32) for n in is_near]) == 1, from_near, from_far)

    def hand_out(c):
        over(c).wait_recv()
        sent_c[c, 0] = parent_of(c, outer_at + 1 - side)
        to_relay(c).start()
        sent_c[c, 1] = parent_of(c, outer_at + side)
        to_outer(c, side).start()
        sent_c[c, 2] = parent_of(c, inner_at + 1 - side)
        to_other(c, side).start()
        sent_c[c, 3] = parent_of(c, own)
        stay(c).start()

    @pl.when(inner)
    def _():
        for c in range(pieces + LAG):
            if c < pieces:
                pass_over(c)
            if c >= LAG:
                hand_out(c - LAG)
        for c in range(pieces):
            stay(c).wait()
            to_other(c, 1 - side).wait_recv()

    @pl.when(outer)
    def _():
        for c in range(pieces):
            to_relay(c).wait_recv()
            relay(c, side).start()
        for c in range(pieces):
            to_outer(c, side).wait_recv()
            relay(c, 1 - side).wait_recv()

    for at_lat in range(2):
        @pl.when(lat == at_lat)
        def _():
            fields_edge(at_lat).start()

    for c in range(pieces):
        for to in range(PAIR):
            @pl.when(jnp.logical_not(inner & (side == to)))
            def _():
                to_inner(c, to, own).wait_send()

    @pl.when(inner)
    def _():
        for c in range(pieces):
            over(c).wait_send()
            to_relay(c).wait_send()
            to_outer(c, side).wait_send()
            to_other(c, side).wait_send()

    @pl.when(outer)
    def _():
        for c in range(pieces):
            relay(c, side).wait_send()

    for at_lat in range(2):
        @pl.when(lat == at_lat)
        def _():
            blank(at_lat).wait()
            for edge in (forced_edge, fields_edge):
                edge(at_lat).wait_send()
                edge(1 - at_lat).wait_recv()


def gather_parents(crossing, ancestors, block, forced):
    fields_count, band_rows, columns = block.shape
    pieces = fields_count * CUTS
    part = (band_rows // PAIR // CUTS, columns)
    edge = jax.ShapeDtypeStruct((fields_count + 1, HALO, columns), jnp.float32)
    return pl.pallas_call(
        functools.partial(gather_kernel, crossing),
        out_shape=[jax.ShapeDtypeStruct(block.shape, jnp.float32), edge, edge],
        in_specs=[pl.BlockSpec(memory_space=pltpu.SMEM)] + [pl.BlockSpec(memory_space=pl.ANY)] * 2,
        out_specs=[pl.BlockSpec(memory_space=pl.ANY)] * 3,
        scratch_shapes=[
            *[pltpu.VMEM((HALF, *part), jnp.float32)] * pieces,
            *[pltpu.VMEM((crossing, *part), jnp.float32)] * pieces,
            pltpu.VMEM((pieces, crossing, *part), jnp.float32),
            pltpu.VMEM((pieces, HALF, *part), jnp.float32),
            pltpu.VMEM((pieces, *part), jnp.float32),
            pltpu.VMEM((fields_count + 1, HALO, columns), jnp.float32),
            pltpu.SemaphoreType.DMA((pieces, PAIR)),
            pltpu.SemaphoreType.DMA((pieces, HALF)),
            pltpu.SemaphoreType.DMA((pieces,)),
            pltpu.SemaphoreType.DMA((pieces,)),
            pltpu.SemaphoreType.DMA((pieces, HALF)),
            pltpu.SemaphoreType.DMA((pieces, PAIR)),
            pltpu.SemaphoreType.DMA((pieces,)),
            pltpu.SemaphoreType.DMA((2,)),
            pltpu.SemaphoreType.DMA((2,)),
            pltpu.SemaphoreType.DMA((1,)),
        ],
        compiler_params=pltpu.CompilerParams(
            collective_id=crossing, has_side_effects=True, vmem_limit_bytes=24 * 1024 * 1024
        ),
        name="gather_parents",
    )(ancestors, block, forced)


def gather_by_halves(block, forced, ancestors):
    groups = lax.axis_size("groups")
    lists = [ancestors] + [
        lax.ppermute(ancestors, "groups", [(i, (i + step) % groups) for i in range(groups)])
        for step in range(1, groups)
    ]
    most = pl.pallas_call(
        functools.partial(other_half_count, groups),
        out_shape=jax.ShapeDtypeStruct((1,), jnp.int32),
        in_specs=[pl.BlockSpec(memory_space=pltpu.SMEM)] * groups,
        out_specs=pl.BlockSpec(memory_space=pltpu.SMEM),
        name="other_half_count",
    )(*lists)[0]
    least = HALF // 2

    def run(crossing):
        return lambda: gather_parents(crossing, ancestors, block, forced)

    return lax.switch(
        jnp.maximum(most - least, 0), [run(crossing) for crossing in range(least, HALF + 1)]
    )


def copy_members(block, ancestors):
    pieces = lax.all_to_all(block, "mem", split_axis=2, concat_axis=0, tiled=True)
    taken = jnp.take(pieces, ancestors, axis=0)
    return lax.all_to_all(taken, "mem", split_axis=0, concat_axis=2, tiled=True)[0]


def edge_rows(values):
    count = lax.axis_size("lat")
    forward = [(i, i + 1) for i in range(count - 1)]
    backward = [(target, source) for source, target in forward]
    low = lax.ppermute(values[:, -HALO:], "lat", forward)
    high = lax.ppermute(values[:, :HALO], "lat", backward)
    return low, high


def on_device(ensemble, forcing_table, ancestors, selector):
    table_edges = jnp.concatenate([forcing_table[:, :HALO], forcing_table[:, -HALO:]], axis=1)
    chosen = lax.dynamic_index_in_dim(table_edges, selector[0], 0)
    by_halves = lax.axis_size("mem") == 2 * HALF and lax.axis_size("lat") == 2
    if by_halves and ensemble.shape[2] % (PAIR * CUTS * HALO) == 0:
        parents, low, high = gather_by_halves(ensemble[0], chosen, ancestors)
    else:
        parents = copy_members(ensemble, ancestors)
        ends = jnp.concatenate([parents[:, :HALO], parents[:, -HALO:]], axis=1)
        low, high = edge_rows(jnp.concatenate([ends, chosen], axis=0))
    return run_window(parents, low, high, forcing_table, selector, lax.axis_size("lat"))[None]


def solution(mesh):
    placed = (
        P(("groups", "mem"), None, "lat", None),
        P(None, "lat", None),
        P("groups"),
        P(("groups", "mem")),
    )
    return jax.shard_map(
        on_device,
        mesh=mesh,
        in_specs=placed,
        out_specs=P(("groups", "mem"), None, "lat", None),
        check_vma=False,
    )
```

```python
import functools

import jax
import jax.numpy as jnp
from jax import lax
from jax.experimental import pallas as pl
from jax.experimental.pallas import tpu as pltpu
from jax.sharding import PartitionSpec as P

STEPS = 3
TIME_STEP = 0.25
DENSITY_RATIO = 0.9
DRAG_RATE = 0.1
CORIOLIS_MEAN = 0.5
HALO = 8
MOST_ROWS = 48


def col_west(values):
    return pltpu.roll(values, 1, axis=2)


def col_east(values):
    return pltpu.roll(values, values.shape[2] - 1, axis=2)


def chunk_rows(rows):
    tiles = rows // HALO
    return HALO * max(n for n in range(1, MOST_ROWS // HALO + 1) if tiles % n == 0)


def window_kernel(lat_count, selector, parents, low, high, table, out, state, other, forcing, sems):
    band_rows, columns = parents.shape[1:]
    chunk = chunk_rows(band_rows + 2 * HALO)
    first = 2 * HALO
    end = first + band_rows
    copies = [
        (parents, state.at[:, pl.ds(first, band_rows)]),
        (low.at[pl.ds(0, 6)], state.at[:, pl.ds(HALO, HALO)]),
        (high.at[pl.ds(0, 6)], state.at[:, pl.ds(end, HALO)]),
        (table.at[selector[0]], forcing.at[pl.ds(first, band_rows)]),
        (low.at[6], forcing.at[pl.ds(HALO, HALO)]),
        (high.at[6], forcing.at[pl.ds(end, HALO)]),
    ]
    copies = [pltpu.make_async_copy(src, dst, sems.at[i]) for i, (src, dst) in enumerate(copies)]
    for copy in copies:
        copy.start()
    for copy in copies:
        copy.wait()

    lat = lax.axis_index("lat")
    base_row = lat * band_rows
    total = band_rows * lat_count
    tiles = chunk // HALO
    row_in_chunk = HALO * lax.broadcasted_iota(
        jnp.int32, (tiles, HALO, 128), 0
    ) + lax.broadcasted_iota(jnp.int32, (tiles, HALO, 128), 1)
    wide_rows = lax.broadcasted_iota(jnp.int32, (tiles, HALO, columns), 1)
    is_first, is_last = wide_rows == 0, wide_rows == HALO - 1

    def spread(values):
        return jnp.concatenate([values] * (columns // 128), axis=-1)

    for field in (2, 5):
        walled = spread((base_row + row_in_chunk[0] >= 1).astype(jnp.float32))
        state[field, first : first + HALO, :] *= walled

    def advance(src, dst, start):
        def at(ref, field, shift=0, count=tiles):
            here = pl.ds(pl.multiple_of(start + shift, HALO), count * HALO)
            return ref[field, here, :].reshape(count, HALO, columns)

        def below(here, ref, field):
            lower = jnp.concatenate([at(ref, field, -HALO, 1), here[:-1]], axis=0)
            return pltpu.roll(jnp.where(is_last, lower, here), 1, axis=1)

        def above(here, ref, field):
            higher = jnp.concatenate([here[1:], at(ref, field, chunk, 1)], axis=0)
            return pltpu.roll(jnp.where(is_first, higher, here), HALO - 1, axis=1)

        def put(field, values):
            dst[field, pl.ds(start, chunk), :] = values.reshape(chunk, columns)

        rows_int = base_row + (start - first) + row_in_chunk
        rows = rows_int.astype(jnp.float32)
        wall = spread(((rows_int >= 1) & (rows_int < total)).astype(jnp.float32))
        coriolis_u = spread(CORIOLIS_MEAN + (rows / total - 0.5))
        coriolis_v = spread(CORIOLIS_MEAN + ((rows - 0.5) / total - 0.5))
        layers = []
        for field in (0, 3):
            height, speed_u, speed_v = at(src, field), at(src, field + 1), at(src, field + 2)
            above_v = above(speed_v, src, field + 2)
            thickness = 1.0 + height
            flux_x = speed_u * (0.5 * (thickness + col_west(thickness)))
            flux_y = speed_v * (0.5 * (thickness + (1.0 + below(height, src, field))))
            flux_y_above = above_v * (0.5 * ((1.0 + above(height, src, field)) + thickness))
            divergence = (col_east(flux_x) - flux_x) + (flux_y_above - flux_y)
            new_height = height - TIME_STEP * divergence
            put(field, new_height)
            layers.append((new_height, speed_u, speed_v, above_v))
        upper, lower = layers[0][0], layers[1][0]
        upper_below, lower_below = below(upper, dst, 0), below(lower, dst, 3)
        pressures = [upper + lower, DENSITY_RATIO * upper + lower]
        pressures_below = [upper_below + lower_below, DENSITY_RATIO * upper_below + lower_below]
        for layer, field in enumerate((0, 3)):
            _, speed_u, speed_v, above_v = layers[layer]
            pressure = pressures[layer]
            if layer == 0:
                extra = forcing[pl.ds(start, chunk), :].reshape(tiles, HALO, columns)
            else:
                extra = -DRAG_RATE * speed_u
            sum_v = speed_v + above_v
            mean_v = 0.25 * (sum_v + col_west(sum_v))
            new_u = speed_u + TIME_STEP * (
                coriolis_u * mean_v - (pressure - col_west(pressure)) + extra
            )
            sum_u = speed_u + below(speed_u, src, field + 1)
            mean_u = 0.25 * (sum_u + col_east(sum_u))
            new_v = speed_v + TIME_STEP * (
                -coriolis_v * mean_u - (pressure - pressures_below[layer])
            )
            put(field + 1, new_u)
            put(field + 2, new_v * wall)

    src, dst = state, other
    for step in range(STEPS):
        def body(index, carry, src=src, dst=dst):
            advance(src, dst, pl.multiple_of(HALO + index * chunk, HALO))
            return carry

        lax.fori_loop(0, (band_rows + 2 * HALO) // chunk, body, 0)
        src, dst = dst, src
    done = pltpu.make_async_copy(src.at[:, pl.ds(first, band_rows)], out, sems.at[0])
    done.start()
    done.wait()


def run_window(parents, low, high, table, selector, lat_count):
    fields_count, band_rows, columns = parents.shape
    held = (fields_count, band_rows + 4 * HALO, columns)
    return pl.pallas_call(
        functools.partial(window_kernel, lat_count),
        out_shape=jax.ShapeDtypeStruct(parents.shape, jnp.float32),
        in_specs=[pl.BlockSpec(memory_space=pltpu.SMEM)] + [pl.BlockSpec(memory_space=pl.ANY)] * 4,
        out_specs=pl.BlockSpec(memory_space=pl.ANY),
        scratch_shapes=[
            pltpu.VMEM(held, jnp.float32),
            pltpu.VMEM(held, jnp.float32),
            pltpu.VMEM(held[1:], jnp.float32),
            pltpu.SemaphoreType.DMA((6,)),
        ],
        compiler_params=pltpu.CompilerParams(vmem_limit_bytes=24 * 1024 * 1024),
        name="window",
    )(selector, parents, low, high, table)


MESH = pl.DeviceIdType.MESH
PAIR = 2
HALF = 2 * PAIR
CUTS = 2
LAG = 2
AHEAD = 2
RELAY_LAG = 6


def other_half_count(lists_count, *refs):
    lists, out = refs[:lists_count], refs[lists_count]
    most = jnp.int32(0)
    for ancestors in lists:
        for half in range(2):
            wanted = [ancestors[half * HALF + s] for s in range(HALF)]
            most = jnp.maximum(most, ranks(wanted, 1 - half)[2])
    out[0] = most


def ranks(wanted, named_half):
    named, rank, before = [], [], jnp.int32(0)
    for m in range(HALF):
        hits = [(one == named_half * HALF + m).astype(jnp.int32) for one in wanted]
        named.append(functools.reduce(jnp.maximum, hits))
        rank.append(before)
        before = before + named[-1]
    return named, rank, before


def gather_kernel(crossing, ancestors, block, forced, out, low, high, *scratch):
    fields_count, band_rows = block.shape[:2]
    pieces = fields_count * CUTS
    part = band_rows // PAIR
    piece_rows = part // CUTS
    near, far = scratch[:pieces], scratch[pieces : 2 * pieces]
    sent_b, sent_c, relayed, zeros = scratch[2 * pieces : 2 * pieces + 4]
    a_send, a_recv, b_send, b_recv, c_send, c_recv, r_recv = scratch[-10:-3]
    e_send, e_recv, local = scratch[-3:]
    mem, lat = lax.axis_index("mem"), lax.axis_index("lat")
    half, own = mem // HALF, mem % HALF
    side = own % PAIR
    inner_at = (1 - half) * PAIR
    outer_at = half * PAIR
    inner = own // PAIR == 1 - half
    outer = jnp.logical_not(inner)
    across = (3 - mem // PAIR) * PAIR + side

    mine = [ancestors[half * HALF + s] for s in range(HALF)]
    theirs = [ancestors[(1 - half) * HALF + s] for s in range(HALF)]
    named, rank, _ = ranks(theirs, half)
    picks = [
        sum(m * named[m] * (rank[m] == j).astype(jnp.int32) for m in range(HALF))
        for j in range(crossing)
    ]
    _, rank, _ = ranks(mine, 1 - half)
    arrived = [
        sum((p == (1 - half) * HALF + m).astype(jnp.int32) * rank[m] for m in range(HALF))
        for p in mine
    ]
    is_near = [p // HALF == half for p in mine]

    def piece(ref, c, which):
        start = which * part + c % CUTS * piece_rows
        return ref.at[c // CUTS, pl.ds(pl.multiple_of(start, HALO), piece_rows)]

    def remote(src, dst, send, recv, target):
        return pltpu.make_async_remote_copy(
            src_ref=src, dst_ref=dst, send_sem=send, recv_sem=recv,
            device_id=target, device_id_type=MESH,
        )

    def slot(local_index):
        return {"mem": half * HALF + local_index}

    def to_inner(c, to, origin):
        return remote(
            piece(block, c, to), near[c].at[origin],
            a_send.at[c, to], a_recv.at[c, origin], slot(inner_at + to),
        )

    def keep(c):
        return pltpu.make_async_copy(piece(block, c, side), near[c].at[own], a_recv.at[c, own])

    def over(c):
        return remote(sent_b.at[c], far[c], b_send.at[c], b_recv.at[c], {"mem": across})

    def to_relay(c):
        return remote(
            sent_c.at[c, 0], relayed.at[c], c_send.at[c, 0], r_recv.at[c], slot(outer_at + side)
        )

    def relay(c, origin):
        return remote(
            relayed.at[c], piece(out, c, origin),
            c_send.at[c, 0], c_recv.at[c, origin], slot(outer_at + 1 - side),
        )

    def to_outer(c, origin):
        return remote(
            sent_c.at[c, 1], piece(out, c, origin),
            c_send.at[c, 1], c_recv.at[c, origin], slot(outer_at + side),
        )

    def to_other(c, origin):
        return remote(
            sent_c.at[c, 2], piece(out, c, origin),
            c_send.at[c, 2], c_recv.at[c, origin], slot(inner_at + 1 - side),
        )

    def stay(c):
        return pltpu.make_async_copy(sent_c.at[c, 3], piece(out, c, side), c_recv.at[c, side])

    barrier = pltpu.get_barrier_semaphore()
    for step in range(1, HALF):
        pl.semaphore_signal(
            barrier, inc=1, device_id=slot((own + step) % HALF), device_id_type=MESH
        )
    pl.semaphore_signal(barrier, inc=1, device_id={"mem": across}, device_id_type=MESH)
    pl.semaphore_signal(barrier, inc=1, device_id={"lat": 1 - lat}, device_id_type=MESH)
    pl.semaphore_wait(barrier, HALF + 1)

    def targets(is_inner):
        return (1 - side,) if is_inner else (side, 1 - side)

    def send(c, is_inner):
        if c < pieces:
            for to in targets(is_inner):
                to_inner(c, to, own).start()

    def sent(c, is_inner):
        for to in targets(is_inner):
            to_inner(c, to, own).wait_send()

    for is_inner, here in ((True, inner), (False, outer)):
        @pl.when(here)
        def _():
            for c in range(AHEAD):
                send(c, is_inner)

    @pl.when(inner)
    def _():
        for c in range(pieces):
            keep(c).start()

    def forced_edge(at_lat):
        first = HALO if at_lat == 0 else 0
        dst = low if at_lat == 0 else high
        return remote(
            forced.at[:, pl.ds(first, HALO)], dst.at[pl.ds(fields_count, 1)],
            e_send.at[0], e_recv.at[0], {"lat": 1 - lat},
        )

    def fields_edge(at_lat):
        first = band_rows - HALO if at_lat == 0 else 0
        dst = low if at_lat == 0 else high
        return remote(
            out.at[:, pl.ds(first, HALO)], dst.at[pl.ds(0, fields_count)],
            e_send.at[1], e_recv.at[1], {"lat": 1 - lat},
        )

    def blank(at_lat):
        return pltpu.make_async_copy(zeros, low if at_lat == 0 else high, local.at[0])

    zeros[...] = jnp.zeros_like(zeros)
    for at_lat in range(2):
        @pl.when(lat == at_lat)
        def _():
            forced_edge(at_lat).start()
            blank(at_lat).start()

    def pass_over(c):
        for origin in range(HALF):
            @pl.when(own == origin)
            def _():
                keep(c).wait()

            @pl.when(own != origin)
            def _():
                to_inner(c, 0, origin).wait_recv()
        for j in range(crossing):
            sent_b[c, j] = near[c][picks[j]]
        over(c).start()
        sent(c, True)
        send(c + AHEAD, True)

    def parent_of(c, local_index):
        def pick(values):
            return sum(
                values[s] * (local_index == s).astype(jnp.int32) for s in range(HALF)
            )

        from_near = near[c][pick([p % HALF for p in mine])]
        from_far = far[c][pick(arrived)]
        return jnp.where(pick([n.astype(jnp.int32) for n in is_near]) == 1, from_near, from_far)

    def hand_out(c):
        over(c).wait_recv()
        sent_c[c, 0] = parent_of(c, outer_at + 1 - side)
        to_relay(c).start()
        sent_c[c, 1] = parent_of(c, outer_at + side)
        to_outer(c, side).start()
        sent_c[c, 2] = parent_of(c, inner_at + 1 - side)
        to_other(c, side).start()
        sent_c[c, 3] = parent_of(c, own)
        stay(c).start()

    @pl.when(inner)
    def _():
        for c in range(pieces + LAG):
            if c < pieces:
                pass_over(c)
            if c >= LAG:
                hand_out(c - LAG)
        for c in range(pieces):
            stay(c).wait()
            to_other(c, 1 - side).wait_recv()

    @pl.when(outer)
    def _():
        for c in range(pieces + RELAY_LAG):
            if c < pieces:
                sent(c, False)
                send(c + AHEAD, False)
            if c >= RELAY_LAG:
                to_relay(c - RELAY_LAG).wait_recv()
                relay(c - RELAY_LAG, side).start()
        for c in range(pieces):
            to_outer(c, side).wait_recv()
            relay(c, 1 - side).wait_recv()

    for at_lat in range(2):
        @pl.when(lat == at_lat)
        def _():
            fields_edge(at_lat).start()

    @pl.when(inner)
    def _():
        for c in range(pieces):
            over(c).wait_send()
            to_relay(c).wait_send()
            to_outer(c, side).wait_send()
            to_other(c, side).wait_send()

    @pl.when(outer)
    def _():
        for c in range(pieces):
            relay(c, side).wait_send()

    for at_lat in range(2):
        @pl.when(lat == at_lat)
        def _():
            blank(at_lat).wait()
            for edge in (forced_edge, fields_edge):
                edge(at_lat).wait_send()
                edge(1 - at_lat).wait_recv()


def gather_parents(crossing, ancestors, block, forced):
    fields_count, band_rows, columns = block.shape
    pieces = fields_count * CUTS
    part = (band_rows // PAIR // CUTS, columns)
    edge = jax.ShapeDtypeStruct((fields_count + 1, HALO, columns), jnp.float32)
    return pl.pallas_call(
        functools.partial(gather_kernel, crossing),
        out_shape=[jax.ShapeDtypeStruct(block.shape, jnp.float32), edge, edge],
        in_specs=[pl.BlockSpec(memory_space=pltpu.SMEM)] + [pl.BlockSpec(memory_space=pl.ANY)] * 2,
        out_specs=[pl.BlockSpec(memory_space=pl.ANY)] * 3,
        scratch_shapes=[
            *[pltpu.VMEM((HALF, *part), jnp.float32)] * pieces,
            *[pltpu.VMEM((crossing, *part), jnp.float32)] * pieces,
            pltpu.VMEM((pieces, crossing, *part), jnp.float32),
            pltpu.VMEM((pieces, HALF, *part), jnp.float32),
            pltpu.VMEM((pieces, *part), jnp.float32),
            pltpu.VMEM((fields_count + 1, HALO, columns), jnp.float32),
            pltpu.SemaphoreType.DMA((pieces, PAIR)),
            pltpu.SemaphoreType.DMA((pieces, HALF)),
            pltpu.SemaphoreType.DMA((pieces,)),
            pltpu.SemaphoreType.DMA((pieces,)),
            pltpu.SemaphoreType.DMA((pieces, HALF)),
            pltpu.SemaphoreType.DMA((pieces, PAIR)),
            pltpu.SemaphoreType.DMA((pieces,)),
            pltpu.SemaphoreType.DMA((2,)),
            pltpu.SemaphoreType.DMA((2,)),
            pltpu.SemaphoreType.DMA((1,)),
        ],
        compiler_params=pltpu.CompilerParams(
            collective_id=crossing, has_side_effects=True, vmem_limit_bytes=24 * 1024 * 1024
        ),
        name="gather_parents",
    )(ancestors, block, forced)


def gather_by_halves(block, forced, ancestors):
    groups = lax.axis_size("groups")
    lists = [ancestors] + [
        lax.ppermute(ancestors, "groups", [(i, (i + step) % groups) for i in range(groups)])
        for step in range(1, groups)
    ]
    most = pl.pallas_call(
        functools.partial(other_half_count, groups),
        out_shape=jax.ShapeDtypeStruct((1,), jnp.int32),
        in_specs=[pl.BlockSpec(memory_space=pltpu.SMEM)] * groups,
        out_specs=pl.BlockSpec(memory_space=pltpu.SMEM),
        name="other_half_count",
    )(*lists)[0]
    least = HALF // 2

    def run(crossing):
        return lambda: gather_parents(crossing, ancestors, block, forced)

    return lax.switch(
        jnp.maximum(most - least, 0), [run(crossing) for crossing in range(least, HALF + 1)]
    )


def copy_members(block, ancestors):
    pieces = lax.all_to_all(block, "mem", split_axis=2, concat_axis=0, tiled=True)
    taken = jnp.take(pieces, ancestors, axis=0)
    return lax.all_to_all(taken, "mem", split_axis=0, concat_axis=2, tiled=True)[0]


def edge_rows(values):
    count = lax.axis_size("lat")
    forward = [(i, i + 1) for i in range(count - 1)]
    backward = [(target, source) for source, target in forward]
    low = lax.ppermute(values[:, -HALO:], "lat", forward)
    high = lax.ppermute(values[:, :HALO], "lat", backward)
    return low, high


def on_device(ensemble, forcing_table, ancestors, selector):
    table_edges = jnp.concatenate([forcing_table[:, :HALO], forcing_table[:, -HALO:]], axis=1)
    chosen = lax.dynamic_index_in_dim(table_edges, selector[0], 0)
    by_halves = lax.axis_size("mem") == 2 * HALF and lax.axis_size("lat") == 2
    if by_halves and ensemble.shape[2] % (PAIR * CUTS * HALO) == 0:
        parents, low, high = gather_by_halves(ensemble[0], chosen, ancestors)
    else:
        parents = copy_members(ensemble, ancestors)
        ends = jnp.concatenate([parents[:, :HALO], parents[:, -HALO:]], axis=1)
        low, high = edge_rows(jnp.concatenate([ends, chosen], axis=0))
    return run_window(parents, low, high, forcing_table, selector, lax.axis_size("lat"))[None]


def solution(mesh):
    placed = (
        P(("groups", "mem"), None, "lat", None),
        P(None, "lat", None),
        P("groups"),
        P(("groups", "mem")),
    )
    return jax.shard_map(
        on_device,
        mesh=mesh,
        in_specs=placed,
        out_specs=P(("groups", "mem"), None, "lat", None),
        check_vma=False,
    )
```

```python
import functools

import jax
import jax.numpy as jnp
from jax import lax
from jax.experimental import pallas as pl
from jax.experimental.pallas import tpu as pltpu
from jax.sharding import PartitionSpec as P

STEPS = 3
TIME_STEP = 0.25
DENSITY_RATIO = 0.9
DRAG_RATE = 0.1
CORIOLIS_MEAN = 0.5
HALO = 8
MOST_ROWS = 48


def col_west(values):
    return pltpu.roll(values, 1, axis=2)


def col_east(values):
    return pltpu.roll(values, values.shape[2] - 1, axis=2)


def chunk_rows(rows):
    tiles = rows // HALO
    return HALO * max(n for n in range(1, MOST_ROWS // HALO + 1) if tiles % n == 0)


def window_kernel(lat_count, selector, parents, low, high, table, out, state, other, forcing, sems):
    band_rows, columns = parents.shape[1:]
    chunk = chunk_rows(band_rows + 2 * HALO)
    first = 2 * HALO
    end = first + band_rows
    copies = [
        (parents, state.at[:, pl.ds(first, band_rows)]),
        (low.at[pl.ds(0, 6)], state.at[:, pl.ds(HALO, HALO)]),
        (high.at[pl.ds(0, 6)], state.at[:, pl.ds(end, HALO)]),
        (table.at[selector[0]], forcing.at[pl.ds(first, band_rows)]),
        (low.at[6 + selector[0]], forcing.at[pl.ds(HALO, HALO)]),
        (high.at[6 + selector[0]], forcing.at[pl.ds(end, HALO)]),
    ]
    copies = [pltpu.make_async_copy(src, dst, sems.at[i]) for i, (src, dst) in enumerate(copies)]
    for copy in copies:
        copy.start()
    for copy in copies:
        copy.wait()

    lat = lax.axis_index("lat")
    base_row = lat * band_rows
    total = band_rows * lat_count
    tiles = chunk // HALO
    row_in_chunk = HALO * lax.broadcasted_iota(
        jnp.int32, (tiles, HALO, 128), 0
    ) + lax.broadcasted_iota(jnp.int32, (tiles, HALO, 128), 1)
    wide_rows = lax.broadcasted_iota(jnp.int32, (tiles, HALO, columns), 1)
    is_first, is_last = wide_rows == 0, wide_rows == HALO - 1

    def spread(values):
        return jnp.concatenate([values] * (columns // 128), axis=-1)

    for start, there in ((HALO, lat > 0), (end, lat < lat_count - 1)):
        rows = pl.ds(start, HALO)
        state[:, rows, :] = jnp.where(there, state[:, rows, :], 0.0)
        forcing[rows, :] = jnp.where(there, forcing[rows, :], 0.0)

    for field in (2, 5):
        walled = spread((base_row + row_in_chunk[0] >= 1).astype(jnp.float32))
        state[field, first : first + HALO, :] *= walled

    def advance(src, dst, start):
        def at(ref, field, shift=0, count=tiles):
            here = pl.ds(pl.multiple_of(start + shift, HALO), count * HALO)
            return ref[field, here, :].reshape(count, HALO, columns)

        def below(here, ref, field):
            lower = jnp.concatenate([at(ref, field, -HALO, 1), here[:-1]], axis=0)
            return pltpu.roll(jnp.where(is_last, lower, here), 1, axis=1)

        def above(here, ref, field):
            higher = jnp.concatenate([here[1:], at(ref, field, chunk, 1)], axis=0)
            return pltpu.roll(jnp.where(is_first, higher, here), HALO - 1, axis=1)

        def put(field, values):
            dst[field, pl.ds(start, chunk), :] = values.reshape(chunk, columns)

        rows_int = base_row + (start - first) + row_in_chunk
        rows = rows_int.astype(jnp.float32)
        wall = spread(((rows_int >= 1) & (rows_int < total)).astype(jnp.float32))
        coriolis_u = spread(CORIOLIS_MEAN + (rows / total - 0.5))
        coriolis_v = spread(CORIOLIS_MEAN + ((rows - 0.5) / total - 0.5))
        layers = []
        for field in (0, 3):
            height, speed_u, speed_v = at(src, field), at(src, field + 1), at(src, field + 2)
            above_v = above(speed_v, src, field + 2)
            thickness = 1.0 + height
            flux_x = speed_u * (0.5 * (thickness + col_west(thickness)))
            flux_y = speed_v * (0.5 * (thickness + (1.0 + below(height, src, field))))
            flux_y_above = above_v * (0.5 * ((1.0 + above(height, src, field)) + thickness))
            divergence = (col_east(flux_x) - flux_x) + (flux_y_above - flux_y)
            new_height = height - TIME_STEP * divergence
            put(field, new_height)
            layers.append((new_height, speed_u, speed_v, above_v))
        upper, lower = layers[0][0], layers[1][0]
        upper_below, lower_below = below(upper, dst, 0), below(lower, dst, 3)
        pressures = [upper + lower, DENSITY_RATIO * upper + lower]
        pressures_below = [upper_below + lower_below, DENSITY_RATIO * upper_below + lower_below]
        for layer, field in enumerate((0, 3)):
            _, speed_u, speed_v, above_v = layers[layer]
            pressure = pressures[layer]
            if layer == 0:
                extra = forcing[pl.ds(start, chunk), :].reshape(tiles, HALO, columns)
            else:
                extra = -DRAG_RATE * speed_u
            sum_v = speed_v + above_v
            mean_v = 0.25 * (sum_v + col_west(sum_v))
            new_u = speed_u + TIME_STEP * (
                coriolis_u * mean_v - (pressure - col_west(pressure)) + extra
            )
            sum_u = speed_u + below(speed_u, src, field + 1)
            mean_u = 0.25 * (sum_u + col_east(sum_u))
            new_v = speed_v + TIME_STEP * (
                -coriolis_v * mean_u - (pressure - pressures_below[layer])
            )
            put(field + 1, new_u)
            put(field + 2, new_v * wall)

    src, dst = state, other
    for step in range(STEPS):
        def body(index, carry, src=src, dst=dst):
            advance(src, dst, pl.multiple_of(HALO + index * chunk, HALO))
            return carry

        lax.fori_loop(0, (band_rows + 2 * HALO) // chunk, body, 0)
        src, dst = dst, src
    done = pltpu.make_async_copy(src.at[:, pl.ds(first, band_rows)], out, sems.at[0])
    done.start()
    done.wait()


def run_window(parents, low, high, table, selector, lat_count):
    fields_count, band_rows, columns = parents.shape
    held = (fields_count, band_rows + 4 * HALO, columns)
    return pl.pallas_call(
        functools.partial(window_kernel, lat_count),
        out_shape=jax.ShapeDtypeStruct(parents.shape, jnp.float32),
        in_specs=[pl.BlockSpec(memory_space=pltpu.SMEM)] + [pl.BlockSpec(memory_space=pl.ANY)] * 4,
        out_specs=pl.BlockSpec(memory_space=pl.ANY),
        scratch_shapes=[
            pltpu.VMEM(held, jnp.float32),
            pltpu.VMEM(held, jnp.float32),
            pltpu.VMEM(held[1:], jnp.float32),
            pltpu.SemaphoreType.DMA((6,)),
        ],
        compiler_params=pltpu.CompilerParams(vmem_limit_bytes=24 * 1024 * 1024),
        name="window",
    )(selector, parents, low, high, table)


MESH = pl.DeviceIdType.MESH
PAIR = 2
HALF = 2 * PAIR
CUTS = 2
LAG = 2
AHEAD = 2


def other_half_count(lists_count, *refs):
    lists, out = refs[:lists_count], refs[lists_count]
    most = jnp.int32(0)
    for ancestors in lists:
        for half in range(2):
            wanted = [ancestors[half * HALF + s] for s in range(HALF)]
            most = jnp.maximum(most, ranks(wanted, 1 - half)[2])
    out[0] = most


def ranks(wanted, named_half):
    named, rank, before = [], [], jnp.int32(0)
    for m in range(HALF):
        hits = [(one == named_half * HALF + m).astype(jnp.int32) for one in wanted]
        named.append(functools.reduce(jnp.maximum, hits))
        rank.append(before)
        before = before + named[-1]
    return named, rank, before


def gather_kernel(crossing, ancestors, block, table, out, edge, *scratch):
    fields_count, band_rows = block.shape[:2]
    pieces = fields_count * CUTS
    part = band_rows // PAIR
    piece_rows = part // CUTS
    near, far = scratch[:pieces], scratch[pieces : 2 * pieces]
    sent_b, sent_c = scratch[2 * pieces : 2 * pieces + 2]
    a_send, a_recv, b_send, b_recv, c_send, c_recv, e_send, e_recv = scratch[-8:]
    mem, lat = lax.axis_index("mem"), lax.axis_index("lat")
    half, own = mem // HALF, mem % HALF
    side = own % PAIR
    inner_at = (1 - half) * PAIR
    outer_at = half * PAIR
    inner = own // PAIR == 1 - half
    outer = jnp.logical_not(inner)
    across = (3 - mem // PAIR) * PAIR + side

    mine = [ancestors[half * HALF + s] for s in range(HALF)]
    theirs = [ancestors[(1 - half) * HALF + s] for s in range(HALF)]
    named, rank, _ = ranks(theirs, half)
    picks = [
        sum(m * named[m] * (rank[m] == j).astype(jnp.int32) for m in range(HALF))
        for j in range(crossing)
    ]
    _, rank, _ = ranks(mine, 1 - half)
    arrived = [
        sum((p == (1 - half) * HALF + m).astype(jnp.int32) * rank[m] for m in range(HALF))
        for p in mine
    ]
    is_near = [p // HALF == half for p in mine]

    def piece(ref, c, which):
        cut = c % CUTS
        start = which * part + jnp.where(lat == 0, CUTS - 1 - cut, cut) * piece_rows
        return ref.at[c // CUTS, pl.ds(pl.multiple_of(start, HALO), piece_rows)]

    def remote(src, dst, send, recv, target):
        return pltpu.make_async_remote_copy(
            src_ref=src, dst_ref=dst, send_sem=send, recv_sem=recv,
            device_id=target, device_id_type=MESH,
        )

    def slot(local_index):
        return {"mem": half * HALF + local_index}

    def to_inner(c, to, origin):
        return remote(
            piece(block, c, to), near[c].at[origin],
            a_send.at[c, to], a_recv.at[c, origin], slot(inner_at + to),
        )

    def keep(c):
        return pltpu.make_async_copy(piece(block, c, side), near[c].at[own], a_recv.at[c, own])

    def over(c):
        return remote(sent_b.at[c], far[c], b_send.at[c], b_recv.at[c], {"mem": across})

    def to_diagonal(c, origin):
        return remote(
            sent_c.at[c, 0], piece(out, c, origin),
            c_send.at[c, 0], c_recv.at[c, origin], slot(outer_at + 1 - side),
        )

    def to_outer(c, origin):
        return remote(
            sent_c.at[c, 1], piece(out, c, origin),
            c_send.at[c, 1], c_recv.at[c, origin], slot(outer_at + side),
        )

    def to_other(c, origin):
        return remote(
            sent_c.at[c, 2], piece(out, c, origin),
            c_send.at[c, 2], c_recv.at[c, origin], slot(inner_at + 1 - side),
        )

    def stay(c):
        return pltpu.make_async_copy(sent_c.at[c, 3], piece(out, c, side), c_recv.at[c, side])

    barrier = pltpu.get_barrier_semaphore()
    for step in range(1, HALF):
        pl.semaphore_signal(
            barrier, inc=1, device_id=slot((own + step) % HALF), device_id_type=MESH
        )
    pl.semaphore_signal(barrier, inc=1, device_id={"mem": across}, device_id_type=MESH)
    pl.semaphore_signal(barrier, inc=1, device_id={"lat": 1 - lat}, device_id_type=MESH)
    pl.semaphore_wait(barrier, HALF + 1)

    def targets(is_inner):
        return (1 - side,) if is_inner else (side, 1 - side)

    def send(c, is_inner):
        if c < pieces:
            for to in targets(is_inner):
                to_inner(c, to, own).start()

    def sent(c, is_inner):
        for to in targets(is_inner):
            to_inner(c, to, own).wait_send()

    for is_inner, here in ((True, inner), (False, outer)):
        @pl.when(here)
        def _():
            for c in range(AHEAD):
                send(c, is_inner)

    @pl.when(inner)
    def _():
        for c in range(pieces):
            keep(c).start()

    def edge_copy(i, at_lat):
        first = band_rows - HALO if at_lat == 0 else 0
        src, place = ((table, fields_count), (out, 0))[i]
        return remote(
            src.at[:, pl.ds(first, HALO)], edge.at[pl.ds(place, src.shape[0])],
            e_send.at[i], e_recv.at[i], {"lat": 1 - lat},
        )

    def start_edge(i):
        for at_lat in range(2):
            @pl.when(lat == at_lat)
            def _():
                edge_copy(i, at_lat).start()

    start_edge(0)

    def pass_over(c):
        for origin in range(HALF):
            @pl.when(own == origin)
            def _():
                keep(c).wait()

            @pl.when(own != origin)
            def _():
                to_inner(c, 0, origin).wait_recv()
        for j in range(crossing):
            sent_b[c, j] = near[c][picks[j]]
        over(c).start()
        sent(c, True)
        send(c + AHEAD, True)

    def parent_of(c, local_index):
        def pick(values):
            return sum(
                values[s] * (local_index == s).astype(jnp.int32) for s in range(HALF)
            )

        from_near = near[c][pick([p % HALF for p in mine])]
        from_far = far[c][pick(arrived)]
        return jnp.where(pick([n.astype(jnp.int32) for n in is_near]) == 1, from_near, from_far)

    def hand_out(c):
        over(c).wait_recv()
        sent_c[c, 0] = parent_of(c, outer_at + 1 - side)
        to_diagonal(c, side).start()
        sent_c[c, 1] = parent_of(c, outer_at + side)
        to_outer(c, side).start()
        sent_c[c, 2] = parent_of(c, inner_at + 1 - side)
        to_other(c, side).start()
        sent_c[c, 3] = parent_of(c, own)
        stay(c).start()

    @pl.when(inner)
    def _():
        for c in range(pieces + LAG):
            if c < pieces:
                pass_over(c)
            if c >= LAG:
                hand_out(c - LAG)

    @pl.when(outer)
    def _():
        for c in range(pieces):
            sent(c, False)
            send(c + AHEAD, False)

    def finish(c):
        @pl.when(inner)
        def _():
            stay(c).wait()
            to_other(c, 1 - side).wait_recv()

        @pl.when(outer)
        def _():
            to_outer(c, side).wait_recv()
            to_diagonal(c, 1 - side).wait_recv()

    for c in range(pieces - 1):
        finish(c)
    start_edge(1)
    finish(pieces - 1)

    @pl.when(inner)
    def _():
        for c in range(pieces):
            over(c).wait_send()
            to_diagonal(c, side).wait_send()
            to_outer(c, side).wait_send()
            to_other(c, side).wait_send()

    for at_lat in range(2):
        @pl.when(lat == at_lat)
        def _():
            for i in range(2):
                edge_copy(i, at_lat).wait_send()
                edge_copy(i, 1 - at_lat).wait_recv()


def gather_parents(crossing, ancestors, block, table):
    fields_count, band_rows, columns = block.shape
    pieces = fields_count * CUTS
    part = (band_rows // PAIR // CUTS, columns)
    edge = jax.ShapeDtypeStruct((fields_count + table.shape[0], HALO, columns), jnp.float32)
    return pl.pallas_call(
        functools.partial(gather_kernel, crossing),
        out_shape=[jax.ShapeDtypeStruct(block.shape, jnp.float32), edge],
        in_specs=[pl.BlockSpec(memory_space=pltpu.SMEM)] + [pl.BlockSpec(memory_space=pl.ANY)] * 2,
        out_specs=[pl.BlockSpec(memory_space=pl.ANY)] * 2,
        scratch_shapes=[
            *[pltpu.VMEM((HALF, *part), jnp.float32)] * pieces,
            *[pltpu.VMEM((crossing, *part), jnp.float32)] * pieces,
            pltpu.VMEM((pieces, crossing, *part), jnp.float32),
            pltpu.VMEM((pieces, HALF, *part), jnp.float32),
            pltpu.SemaphoreType.DMA((pieces, PAIR)),
            pltpu.SemaphoreType.DMA((pieces, HALF)),
            pltpu.SemaphoreType.DMA((pieces,)),
            pltpu.SemaphoreType.DMA((pieces,)),
            pltpu.SemaphoreType.DMA((pieces, HALF)),
            pltpu.SemaphoreType.DMA((pieces, PAIR)),
            pltpu.SemaphoreType.DMA((2,)),
            pltpu.SemaphoreType.DMA((2,)),
        ],
        compiler_params=pltpu.CompilerParams(
            collective_id=crossing, has_side_effects=True, vmem_limit_bytes=24 * 1024 * 1024
        ),
        name="gather_parents",
    )(ancestors, block, table)


def gather_by_halves(block, table, ancestors):
    groups = lax.axis_size("groups")
    lists = [ancestors] + [
        lax.ppermute(ancestors, "groups", [(i, (i + step) % groups) for i in range(groups)])
        for step in range(1, groups)
    ]
    most = pl.pallas_call(
        functools.partial(other_half_count, groups),
        out_shape=jax.ShapeDtypeStruct((1,), jnp.int32),
        in_specs=[pl.BlockSpec(memory_space=pltpu.SMEM)] * groups,
        out_specs=pl.BlockSpec(memory_space=pltpu.SMEM),
        name="other_half_count",
    )(*lists)[0]
    least = HALF // 2

    def run(crossing):
        return lambda: gather_parents(crossing, ancestors, block, table)

    return lax.switch(
        jnp.maximum(most - least, 0), [run(crossing) for crossing in range(least, HALF + 1)]
    )


def copy_members(block, ancestors):
    pieces = lax.all_to_all(block, "mem", split_axis=2, concat_axis=0, tiled=True)
    taken = jnp.take(pieces, ancestors, axis=0)
    return lax.all_to_all(taken, "mem", split_axis=0, concat_axis=2, tiled=True)[0]


def edge_rows(values):
    count = lax.axis_size("lat")
    forward = [(i, i + 1) for i in range(count - 1)]
    backward = [(target, source) for source, target in forward]
    low = lax.ppermute(values[:, -HALO:], "lat", forward)
    high = lax.ppermute(values[:, :HALO], "lat", backward)
    return low, high


def on_device(ensemble, forcing_table, ancestors, selector):
    by_halves = lax.axis_size("mem") == 2 * HALF and lax.axis_size("lat") == 2
    if by_halves and ensemble.shape[2] % (PAIR * CUTS * HALO) == 0:
        parents, edge = gather_by_halves(ensemble[0], forcing_table, ancestors)
        low, high = edge, edge
    else:
        parents = copy_members(ensemble, ancestors)
        ends = [
            jnp.concatenate([values[:, :HALO], values[:, -HALO:]], axis=1)
            for values in (parents, forcing_table)
        ]
        low, high = edge_rows(jnp.concatenate(ends, axis=0))
    return run_window(parents, low, high, forcing_table, selector, lax.axis_size("lat"))[None]


def solution(mesh):
    placed = (
        P(("groups", "mem"), None, "lat", None),
        P(None, "lat", None),
        P("groups"),
        P(("groups", "mem")),
    )
    return jax.shard_map(
        on_device,
        mesh=mesh,
        in_specs=placed,
        out_specs=P(("groups", "mem"), None, "lat", None),
        check_vma=False,
    )
```

```python
import functools

import jax
import jax.numpy as jnp
from jax import lax
from jax.experimental import pallas as pl
from jax.experimental.pallas import tpu as pltpu
from jax.sharding import PartitionSpec as P

STEPS = 3
TIME_STEP = 0.25
DENSITY_RATIO = 0.9
DRAG_RATE = 0.1
CORIOLIS_MEAN = 0.5
HALO = 8
MOST_ROWS = 48


def col_west(values):
    return pltpu.roll(values, 1, axis=2)


def col_east(values):
    return pltpu.roll(values, values.shape[2] - 1, axis=2)


def chunk_rows(rows):
    tiles = rows // HALO
    return HALO * max(n for n in range(1, MOST_ROWS // HALO + 1) if tiles % n == 0)


def window_kernel(lat_count, selector, parents, low, high, table, out, state, other, forcing, sems):
    band_rows, columns = parents.shape[1:]
    chunk = chunk_rows(band_rows + 2 * HALO)
    first = 2 * HALO
    end = first + band_rows
    copies = [
        (parents, state.at[:, pl.ds(first, band_rows)]),
        (low.at[pl.ds(0, 6)], state.at[:, pl.ds(HALO, HALO)]),
        (high.at[pl.ds(0, 6)], state.at[:, pl.ds(end, HALO)]),
        (table.at[selector[0]], forcing.at[pl.ds(first, band_rows)]),
        (low.at[6 + selector[0]], forcing.at[pl.ds(HALO, HALO)]),
        (high.at[6 + selector[0]], forcing.at[pl.ds(end, HALO)]),
    ]
    copies = [pltpu.make_async_copy(src, dst, sems.at[i]) for i, (src, dst) in enumerate(copies)]
    for copy in copies:
        copy.start()
    for copy in copies:
        copy.wait()

    lat = lax.axis_index("lat")
    base_row = lat * band_rows
    total = band_rows * lat_count
    tiles = chunk // HALO
    row_in_chunk = HALO * lax.broadcasted_iota(
        jnp.int32, (tiles, HALO, 128), 0
    ) + lax.broadcasted_iota(jnp.int32, (tiles, HALO, 128), 1)
    wide_rows = lax.broadcasted_iota(jnp.int32, (tiles, HALO, columns), 1)
    is_first, is_last = wide_rows == 0, wide_rows == HALO - 1

    def spread(values):
        return jnp.concatenate([values] * (columns // 128), axis=-1)

    for start, there in ((HALO, lat > 0), (end, lat < lat_count - 1)):
        rows = pl.ds(start, HALO)
        state[:, rows, :] = jnp.where(there, state[:, rows, :], 0.0)
        forcing[rows, :] = jnp.where(there, forcing[rows, :], 0.0)

    for field in (2, 5):
        walled = spread((base_row + row_in_chunk[0] >= 1).astype(jnp.float32))
        state[field, first : first + HALO, :] *= walled

    def advance(src, dst, start):
        def at(ref, field, shift=0, count=tiles):
            here = pl.ds(pl.multiple_of(start + shift, HALO), count * HALO)
            return ref[field, here, :].reshape(count, HALO, columns)

        def below(here, ref, field):
            lower = jnp.concatenate([at(ref, field, -HALO, 1), here[:-1]], axis=0)
            return pltpu.roll(jnp.where(is_last, lower, here), 1, axis=1)

        def above(here, ref, field):
            higher = jnp.concatenate([here[1:], at(ref, field, chunk, 1)], axis=0)
            return pltpu.roll(jnp.where(is_first, higher, here), HALO - 1, axis=1)

        def put(field, values):
            dst[field, pl.ds(start, chunk), :] = values.reshape(chunk, columns)

        rows_int = base_row + (start - first) + row_in_chunk
        rows = rows_int.astype(jnp.float32)
        wall = spread(((rows_int >= 1) & (rows_int < total)).astype(jnp.float32))
        coriolis_u = spread(CORIOLIS_MEAN + (rows / total - 0.5))
        coriolis_v = spread(CORIOLIS_MEAN + ((rows - 0.5) / total - 0.5))
        layers = []
        for field in (0, 3):
            height, speed_u, speed_v = at(src, field), at(src, field + 1), at(src, field + 2)
            above_v = above(speed_v, src, field + 2)
            thickness = 1.0 + height
            flux_x = speed_u * (0.5 * (thickness + col_west(thickness)))
            flux_y = speed_v * (0.5 * (thickness + (1.0 + below(height, src, field))))
            flux_y_above = above_v * (0.5 * ((1.0 + above(height, src, field)) + thickness))
            divergence = (col_east(flux_x) - flux_x) + (flux_y_above - flux_y)
            new_height = height - TIME_STEP * divergence
            put(field, new_height)
            layers.append((new_height, speed_u, speed_v, above_v))
        upper, lower = layers[0][0], layers[1][0]
        upper_below, lower_below = below(upper, dst, 0), below(lower, dst, 3)
        pressures = [upper + lower, DENSITY_RATIO * upper + lower]
        pressures_below = [upper_below + lower_below, DENSITY_RATIO * upper_below + lower_below]
        for layer, field in enumerate((0, 3)):
            _, speed_u, speed_v, above_v = layers[layer]
            pressure = pressures[layer]
            if layer == 0:
                extra = forcing[pl.ds(start, chunk), :].reshape(tiles, HALO, columns)
            else:
                extra = -DRAG_RATE * speed_u
            sum_v = speed_v + above_v
            mean_v = 0.25 * (sum_v + col_west(sum_v))
            new_u = speed_u + TIME_STEP * (
                coriolis_u * mean_v - (pressure - col_west(pressure)) + extra
            )
            sum_u = speed_u + below(speed_u, src, field + 1)
            mean_u = 0.25 * (sum_u + col_east(sum_u))
            new_v = speed_v + TIME_STEP * (
                -coriolis_v * mean_u - (pressure - pressures_below[layer])
            )
            put(field + 1, new_u)
            put(field + 2, new_v * wall)

    src, dst = state, other
    for step in range(STEPS):
        def body(index, carry, src=src, dst=dst):
            advance(src, dst, pl.multiple_of(HALO + index * chunk, HALO))
            return carry

        lax.fori_loop(0, (band_rows + 2 * HALO) // chunk, body, 0)
        src, dst = dst, src
    done = pltpu.make_async_copy(src.at[:, pl.ds(first, band_rows)], out, sems.at[0])
    done.start()
    done.wait()


def run_window(parents, low, high, table, selector, lat_count):
    fields_count, band_rows, columns = parents.shape
    held = (fields_count, band_rows + 4 * HALO, columns)
    return pl.pallas_call(
        functools.partial(window_kernel, lat_count),
        out_shape=jax.ShapeDtypeStruct(parents.shape, jnp.float32),
        in_specs=[pl.BlockSpec(memory_space=pltpu.SMEM)] + [pl.BlockSpec(memory_space=pl.ANY)] * 4,
        out_specs=pl.BlockSpec(memory_space=pl.ANY),
        scratch_shapes=[
            pltpu.VMEM(held, jnp.float32),
            pltpu.VMEM(held, jnp.float32),
            pltpu.VMEM(held[1:], jnp.float32),
            pltpu.SemaphoreType.DMA((6,)),
        ],
        compiler_params=pltpu.CompilerParams(vmem_limit_bytes=24 * 1024 * 1024),
        name="window",
    )(selector, parents, low, high, table)


MESH = pl.DeviceIdType.MESH
PAIR = 2
HALF = 2 * PAIR
CUTS = 2
LAG = 1
AHEAD = 3
RELAY_LAG = 6


def other_half_count(lists_count, *refs):
    lists, out = refs[:lists_count], refs[lists_count]
    most = jnp.int32(0)
    for ancestors in lists:
        for half in range(2):
            wanted = [ancestors[half * HALF + s] for s in range(HALF)]
            most = jnp.maximum(most, ranks(wanted, 1 - half)[2])
    out[0] = most


def ranks(wanted, named_half):
    named, rank, before = [], [], jnp.int32(0)
    for m in range(HALF):
        hits = [(one == named_half * HALF + m).astype(jnp.int32) for one in wanted]
        named.append(functools.reduce(jnp.maximum, hits))
        rank.append(before)
        before = before + named[-1]
    return named, rank, before


def gather_kernel(crossing, ancestors, block, table, out, edge, *scratch):
    fields_count, band_rows = block.shape[:2]
    pieces = fields_count * CUTS
    part = band_rows // PAIR
    piece_rows = part // CUTS
    near, far = scratch[:pieces], scratch[pieces : 2 * pieces]
    sent_b, sent_c, relayed = scratch[2 * pieces : 2 * pieces + 3]
    a_send, a_recv, b_send, b_recv, c_send, c_recv = scratch[-9:-3]
    r_recv, e_send, e_recv = scratch[-3:]
    mem, lat = lax.axis_index("mem"), lax.axis_index("lat")
    half, own = mem // HALF, mem % HALF
    side = own % PAIR
    inner_at = (1 - half) * PAIR
    outer_at = half * PAIR
    inner = own // PAIR == 1 - half
    outer = jnp.logical_not(inner)
    across = (3 - mem // PAIR) * PAIR + side

    mine = [ancestors[half * HALF + s] for s in range(HALF)]
    theirs = [ancestors[(1 - half) * HALF + s] for s in range(HALF)]
    named, rank, _ = ranks(theirs, half)
    picks = [
        sum(m * named[m] * (rank[m] == j).astype(jnp.int32) for m in range(HALF))
        for j in range(crossing)
    ]
    _, rank, _ = ranks(mine, 1 - half)
    arrived = [
        sum((p == (1 - half) * HALF + m).astype(jnp.int32) * rank[m] for m in range(HALF))
        for p in mine
    ]
    is_near = [p // HALF == half for p in mine]

    def piece(ref, c, which):
        cut = c % CUTS
        start = which * part + jnp.where(lat == 0, CUTS - 1 - cut, cut) * piece_rows
        return ref.at[c // CUTS, pl.ds(pl.multiple_of(start, HALO), piece_rows)]

    def remote(src, dst, send, recv, target):
        return pltpu.make_async_remote_copy(
            src_ref=src, dst_ref=dst, send_sem=send, recv_sem=recv,
            device_id=target, device_id_type=MESH,
        )

    def slot(local_index):
        return {"mem": half * HALF + local_index}

    def to_inner(c, to, origin):
        return remote(
            piece(block, c, to), near[c].at[origin],
            a_send.at[c, to], a_recv.at[c, origin], slot(inner_at + to),
        )

    def keep(c):
        return pltpu.make_async_copy(piece(block, c, side), near[c].at[own], a_recv.at[c, own])

    def over(c):
        return remote(sent_b.at[c], far[c], b_send.at[c], b_recv.at[c], {"mem": across})

    def to_relay(c):
        return remote(
            sent_c.at[c, 0], relayed.at[c], c_send.at[c, 0], r_recv.at[c], slot(outer_at + side)
        )

    def relay(c, origin):
        return remote(
            relayed.at[c], piece(out, c, origin),
            c_send.at[c, 0], c_recv.at[c, origin], slot(outer_at + 1 - side),
        )

    def to_outer(c, origin):
        return remote(
            sent_c.at[c, 1], piece(out, c, origin),
            c_send.at[c, 1], c_recv.at[c, origin], slot(outer_at + side),
        )

    def to_other(c, origin):
        return remote(
            sent_c.at[c, 2], piece(out, c, origin),
            c_send.at[c, 2], c_recv.at[c, origin], slot(inner_at + 1 - side),
        )

    def stay(c):
        return pltpu.make_async_copy(sent_c.at[c, 3], piece(out, c, side), c_recv.at[c, side])

    barrier = pltpu.get_barrier_semaphore()
    for step in range(1, HALF):
        pl.semaphore_signal(
            barrier, inc=1, device_id=slot((own + step) % HALF), device_id_type=MESH
        )
    pl.semaphore_signal(barrier, inc=1, device_id={"mem": across}, device_id_type=MESH)
    pl.semaphore_signal(barrier, inc=1, device_id={"lat": 1 - lat}, device_id_type=MESH)
    pl.semaphore_wait(barrier, HALF + 1)

    def targets(is_inner):
        return (1 - side,) if is_inner else (side, 1 - side)

    def send(c, is_inner):
        if c < pieces:
            for to in targets(is_inner):
                to_inner(c, to, own).start()

    def sent(c, is_inner):
        for to in targets(is_inner):
            to_inner(c, to, own).wait_send()

    for is_inner, here in ((True, inner), (False, outer)):
        @pl.when(here)
        def _():
            for c in range(pieces if is_inner else AHEAD):
                send(c, is_inner)

    @pl.when(inner)
    def _():
        for c in range(pieces):
            keep(c).start()

    def edge_copy(i, at_lat):
        first = band_rows - HALO if at_lat == 0 else 0
        src, place = ((table, fields_count), (out, 0))[i]
        return remote(
            src.at[:, pl.ds(first, HALO)], edge.at[pl.ds(place, src.shape[0])],
            e_send.at[i], e_recv.at[i], {"lat": 1 - lat},
        )

    def start_edge(i):
        for at_lat in range(2):
            @pl.when(lat == at_lat)
            def _():
                edge_copy(i, at_lat).start()

    start_edge(0)

    def pass_over(c):
        for origin in range(HALF):
            @pl.when(own == origin)
            def _():
                keep(c).wait()

            @pl.when(own != origin)
            def _():
                to_inner(c, 0, origin).wait_recv()
        for j in range(crossing):
            sent_b[c, j] = near[c][picks[j]]
        over(c).start()

    def parent_of(c, local_index):
        def pick(values):
            return sum(
                values[s] * (local_index == s).astype(jnp.int32) for s in range(HALF)
            )

        from_near = near[c][pick([p % HALF for p in mine])]
        from_far = far[c][pick(arrived)]
        return jnp.where(pick([n.astype(jnp.int32) for n in is_near]) == 1, from_near, from_far)

    def hand_out(c):
        over(c).wait_recv()
        sent_c[c, 0] = parent_of(c, outer_at + 1 - side)
        to_relay(c).start()
        sent_c[c, 1] = parent_of(c, outer_at + side)
        to_outer(c, side).start()
        sent_c[c, 2] = parent_of(c, inner_at + 1 - side)
        to_other(c, side).start()
        sent_c[c, 3] = parent_of(c, own)
        stay(c).start()

    @pl.when(inner)
    def _():
        for c in range(pieces + LAG):
            if c < pieces:
                pass_over(c)
            if c >= LAG:
                hand_out(c - LAG)

    @pl.when(outer)
    def _():
        for c in range(pieces + RELAY_LAG):
            if c < pieces:
                sent(c, False)
                send(c + AHEAD, False)
            if c >= RELAY_LAG:
                to_relay(c - RELAY_LAG).wait_recv()
                relay(c - RELAY_LAG, side).start()

    def finish(c):
        @pl.when(inner)
        def _():
            stay(c).wait()
            to_other(c, 1 - side).wait_recv()

        @pl.when(outer)
        def _():
            to_outer(c, side).wait_recv()
            relay(c, 1 - side).wait_recv()

    for c in range(pieces - 1):
        finish(c)
    start_edge(1)
    finish(pieces - 1)

    @pl.when(inner)
    def _():
        for c in range(pieces):
            sent(c, True)
            over(c).wait_send()
            to_relay(c).wait_send()
            to_outer(c, side).wait_send()
            to_other(c, side).wait_send()

    @pl.when(outer)
    def _():
        for c in range(pieces):
            relay(c, side).wait_send()

    for at_lat in range(2):
        @pl.when(lat == at_lat)
        def _():
            for i in range(2):
                edge_copy(i, at_lat).wait_send()
                edge_copy(i, 1 - at_lat).wait_recv()


def gather_parents(crossing, ancestors, block, table):
    fields_count, band_rows, columns = block.shape
    pieces = fields_count * CUTS
    part = (band_rows // PAIR // CUTS, columns)
    edge = jax.ShapeDtypeStruct((fields_count + table.shape[0], HALO, columns), jnp.float32)
    return pl.pallas_call(
        functools.partial(gather_kernel, crossing),
        out_shape=[jax.ShapeDtypeStruct(block.shape, jnp.float32), edge],
        in_specs=[pl.BlockSpec(memory_space=pltpu.SMEM)] + [pl.BlockSpec(memory_space=pl.ANY)] * 2,
        out_specs=[pl.BlockSpec(memory_space=pl.ANY)] * 2,
        scratch_shapes=[
            *[pltpu.VMEM((HALF, *part), jnp.float32)] * pieces,
            *[pltpu.VMEM((crossing, *part), jnp.float32)] * pieces,
            pltpu.VMEM((pieces, crossing, *part), jnp.float32),
            pltpu.VMEM((pieces, HALF, *part), jnp.float32),
            pltpu.VMEM((pieces, *part), jnp.float32),
            pltpu.SemaphoreType.DMA((pieces, PAIR)),
            pltpu.SemaphoreType.DMA((pieces, HALF)),
            pltpu.SemaphoreType.DMA((pieces,)),
            pltpu.SemaphoreType.DMA((pieces,)),
            pltpu.SemaphoreType.DMA((pieces, HALF)),
            pltpu.SemaphoreType.DMA((pieces, PAIR)),
            pltpu.SemaphoreType.DMA((pieces,)),
            pltpu.SemaphoreType.DMA((2,)),
            pltpu.SemaphoreType.DMA((2,)),
        ],
        compiler_params=pltpu.CompilerParams(
            collective_id=crossing, has_side_effects=True, vmem_limit_bytes=24 * 1024 * 1024
        ),
        name="gather_parents",
    )(ancestors, block, table)


def gather_by_halves(block, table, ancestors):
    groups = lax.axis_size("groups")
    lists = [ancestors] + [
        lax.ppermute(ancestors, "groups", [(i, (i + step) % groups) for i in range(groups)])
        for step in range(1, groups)
    ]
    most = pl.pallas_call(
        functools.partial(other_half_count, groups),
        out_shape=jax.ShapeDtypeStruct((1,), jnp.int32),
        in_specs=[pl.BlockSpec(memory_space=pltpu.SMEM)] * groups,
        out_specs=pl.BlockSpec(memory_space=pltpu.SMEM),
        name="other_half_count",
    )(*lists)[0]
    least = HALF // 2

    def run(crossing):
        return lambda: gather_parents(crossing, ancestors, block, table)

    return lax.switch(
        jnp.maximum(most - least, 0), [run(crossing) for crossing in range(least, HALF + 1)]
    )


def copy_members(block, ancestors):
    pieces = lax.all_to_all(block, "mem", split_axis=2, concat_axis=0, tiled=True)
    taken = jnp.take(pieces, ancestors, axis=0)
    return lax.all_to_all(taken, "mem", split_axis=0, concat_axis=2, tiled=True)[0]


def edge_rows(values):
    count = lax.axis_size("lat")
    forward = [(i, i + 1) for i in range(count - 1)]
    backward = [(target, source) for source, target in forward]
    low = lax.ppermute(values[:, -HALO:], "lat", forward)
    high = lax.ppermute(values[:, :HALO], "lat", backward)
    return low, high


def on_device(ensemble, forcing_table, ancestors, selector):
    by_halves = lax.axis_size("mem") == 2 * HALF and lax.axis_size("lat") == 2
    if by_halves and ensemble.shape[2] % (PAIR * CUTS * HALO) == 0:
        parents, edge = gather_by_halves(ensemble[0], forcing_table, ancestors)
        low, high = edge, edge
    else:
        parents = copy_members(ensemble, ancestors)
        ends = [
            jnp.concatenate([values[:, :HALO], values[:, -HALO:]], axis=1)
            for values in (parents, forcing_table)
        ]
        low, high = edge_rows(jnp.concatenate(ends, axis=0))
    return run_window(parents, low, high, forcing_table, selector, lax.axis_size("lat"))[None]


def solution(mesh):
    placed = (
        P(("groups", "mem"), None, "lat", None),
        P(None, "lat", None),
        P("groups"),
        P(("groups", "mem")),
    )
    return jax.shard_map(
        on_device,
        mesh=mesh,
        in_specs=placed,
        out_specs=P(("groups", "mem"), None, "lat", None),
        check_vma=False,
    )
```

```python
import functools

import jax
import jax.numpy as jnp
from jax import lax
from jax.experimental import pallas as pl
from jax.experimental.pallas import tpu as pltpu
from jax.sharding import PartitionSpec as P

STEPS = 3
TIME_STEP = 0.25
DENSITY_RATIO = 0.9
DRAG_RATE = 0.1
CORIOLIS_MEAN = 0.5
HALO = 8
MOST_ROWS = 72


def col_west(values):
    return pltpu.roll(values, 1, axis=2)


def col_east(values):
    return pltpu.roll(values, values.shape[2] - 1, axis=2)


def chunk_rows(rows):
    tiles = rows // HALO
    return HALO * max(n for n in range(1, MOST_ROWS // HALO + 1) if tiles % n == 0)


def window_kernel(lat_count, selector, parents, low, high, table, out, state, other, forcing, sems):
    band_rows, columns = parents.shape[1:]
    chunk = chunk_rows(band_rows + 2 * HALO)
    first = 2 * HALO
    end = first + band_rows
    copies = [
        (parents, state.at[:, pl.ds(first, band_rows)]),
        (low.at[pl.ds(0, 6)], state.at[:, pl.ds(HALO, HALO)]),
        (high.at[pl.ds(0, 6)], state.at[:, pl.ds(end, HALO)]),
        (table.at[selector[0]], forcing.at[pl.ds(first, band_rows)]),
        (low.at[6 + selector[0]], forcing.at[pl.ds(HALO, HALO)]),
        (high.at[6 + selector[0]], forcing.at[pl.ds(end, HALO)]),
    ]
    copies = [pltpu.make_async_copy(src, dst, sems.at[i]) for i, (src, dst) in enumerate(copies)]
    for copy in copies:
        copy.start()
    for copy in copies:
        copy.wait()

    lat = lax.axis_index("lat")
    base_row = lat * band_rows
    total = band_rows * lat_count
    tiles = chunk // HALO
    row_in_chunk = HALO * lax.broadcasted_iota(
        jnp.int32, (tiles, HALO, 128), 0
    ) + lax.broadcasted_iota(jnp.int32, (tiles, HALO, 128), 1)
    wide_rows = lax.broadcasted_iota(jnp.int32, (tiles, HALO, columns), 1)
    is_first, is_last = wide_rows == 0, wide_rows == HALO - 1

    def spread(values):
        return jnp.concatenate([values] * (columns // 128), axis=-1)

    for start, there in ((HALO, lat > 0), (end, lat < lat_count - 1)):
        rows = pl.ds(start, HALO)
        state[:, rows, :] = jnp.where(there, state[:, rows, :], 0.0)
        forcing[rows, :] = jnp.where(there, forcing[rows, :], 0.0)

    for field in (2, 5):
        walled = spread((base_row + row_in_chunk[0] >= 1).astype(jnp.float32))
        state[field, first : first + HALO, :] *= walled

    def advance(src, dst, start):
        def at(ref, field, shift=0, count=tiles):
            here = pl.ds(pl.multiple_of(start + shift, HALO), count * HALO)
            return ref[field, here, :].reshape(count, HALO, columns)

        def below(here, ref, field):
            lower = jnp.concatenate([at(ref, field, -HALO, 1), here[:-1]], axis=0)
            return pltpu.roll(jnp.where(is_last, lower, here), 1, axis=1)

        def above(here, ref, field):
            higher = jnp.concatenate([here[1:], at(ref, field, chunk, 1)], axis=0)
            return pltpu.roll(jnp.where(is_first, higher, here), HALO - 1, axis=1)

        def put(field, values):
            dst[field, pl.ds(start, chunk), :] = values.reshape(chunk, columns)

        rows_int = base_row + (start - first) + row_in_chunk
        rows = rows_int.astype(jnp.float32)
        wall = spread(((rows_int >= 1) & (rows_int < total)).astype(jnp.float32))
        coriolis_u = spread(CORIOLIS_MEAN + (rows / total - 0.5))
        coriolis_v = spread(CORIOLIS_MEAN + ((rows - 0.5) / total - 0.5))
        layers = []
        for field in (0, 3):
            height, speed_u, speed_v = at(src, field), at(src, field + 1), at(src, field + 2)
            above_v = above(speed_v, src, field + 2)
            thickness = 1.0 + height
            flux_x = speed_u * (0.5 * (thickness + col_west(thickness)))
            flux_y = speed_v * (0.5 * (thickness + (1.0 + below(height, src, field))))
            flux_y_above = above_v * (0.5 * ((1.0 + above(height, src, field)) + thickness))
            divergence = (col_east(flux_x) - flux_x) + (flux_y_above - flux_y)
            new_height = height - TIME_STEP * divergence
            put(field, new_height)
            layers.append((new_height, speed_u, speed_v, above_v))
        upper, lower = layers[0][0], layers[1][0]
        upper_below, lower_below = below(upper, dst, 0), below(lower, dst, 3)
        pressures = [upper + lower, DENSITY_RATIO * upper + lower]
        pressures_below = [upper_below + lower_below, DENSITY_RATIO * upper_below + lower_below]
        for layer, field in enumerate((0, 3)):
            _, speed_u, speed_v, above_v = layers[layer]
            pressure = pressures[layer]
            if layer == 0:
                extra = forcing[pl.ds(start, chunk), :].reshape(tiles, HALO, columns)
            else:
                extra = -DRAG_RATE * speed_u
            sum_v = speed_v + above_v
            mean_v = 0.25 * (sum_v + col_west(sum_v))
            new_u = speed_u + TIME_STEP * (
                coriolis_u * mean_v - (pressure - col_west(pressure)) + extra
            )
            sum_u = speed_u + below(speed_u, src, field + 1)
            mean_u = 0.25 * (sum_u + col_east(sum_u))
            new_v = speed_v + TIME_STEP * (
                -coriolis_v * mean_u - (pressure - pressures_below[layer])
            )
            put(field + 1, new_u)
            put(field + 2, new_v * wall)

    src, dst = state, other
    for step in range(STEPS):
        def body(index, carry, src=src, dst=dst):
            advance(src, dst, pl.multiple_of(HALO + index * chunk, HALO))
            return carry

        lax.fori_loop(0, (band_rows + 2 * HALO) // chunk, body, 0)
        src, dst = dst, src
    done = pltpu.make_async_copy(src.at[:, pl.ds(first, band_rows)], out, sems.at[0])
    done.start()
    done.wait()


def run_window(parents, low, high, table, selector, lat_count):
    fields_count, band_rows, columns = parents.shape
    held = (fields_count, band_rows + 4 * HALO, columns)
    return pl.pallas_call(
        functools.partial(window_kernel, lat_count),
        out_shape=jax.ShapeDtypeStruct(parents.shape, jnp.float32),
        in_specs=[pl.BlockSpec(memory_space=pltpu.SMEM)] + [pl.BlockSpec(memory_space=pl.ANY)] * 4,
        out_specs=pl.BlockSpec(memory_space=pl.ANY),
        scratch_shapes=[
            pltpu.VMEM(held, jnp.float32),
            pltpu.VMEM(held, jnp.float32),
            pltpu.VMEM(held[1:], jnp.float32),
            pltpu.SemaphoreType.DMA((6,)),
        ],
        compiler_params=pltpu.CompilerParams(vmem_limit_bytes=24 * 1024 * 1024),
        name="window",
    )(selector, parents, low, high, table)


MESH = pl.DeviceIdType.MESH
PAIR = 2
HALF = 2 * PAIR
CUTS = 2
LAG = 1
AHEAD = 3
RELAY_LAG = 6


def other_half_count(lists_count, *refs):
    lists, out = refs[:lists_count], refs[lists_count]
    most = jnp.int32(0)
    for ancestors in lists:
        for half in range(2):
            wanted = [ancestors[half * HALF + s] for s in range(HALF)]
            most = jnp.maximum(most, ranks(wanted, 1 - half)[2])
    out[0] = most


def ranks(wanted, named_half):
    named, rank, before = [], [], jnp.int32(0)
    for m in range(HALF):
        hits = [(one == named_half * HALF + m).astype(jnp.int32) for one in wanted]
        named.append(functools.reduce(jnp.maximum, hits))
        rank.append(before)
        before = before + named[-1]
    return named, rank, before


def gather_kernel(crossing, ancestors, block, table, out, edge, *scratch):
    fields_count, band_rows = block.shape[:2]
    pieces = fields_count * CUTS
    part = band_rows // PAIR
    piece_rows = part // CUTS
    near, far = scratch[:pieces], scratch[pieces : 2 * pieces]
    sent_b, sent_c, relayed = scratch[2 * pieces : 2 * pieces + 3]
    a_send, a_recv, b_send, b_recv, c_send, c_recv = scratch[-9:-3]
    r_recv, e_send, e_recv = scratch[-3:]
    mem, lat = lax.axis_index("mem"), lax.axis_index("lat")
    half, own = mem // HALF, mem % HALF
    side = own % PAIR
    inner_at = (1 - half) * PAIR
    outer_at = half * PAIR
    inner = own // PAIR == 1 - half
    outer = jnp.logical_not(inner)
    across = (3 - mem // PAIR) * PAIR + side

    mine = [ancestors[half * HALF + s] for s in range(HALF)]
    theirs = [ancestors[(1 - half) * HALF + s] for s in range(HALF)]
    named, rank, _ = ranks(theirs, half)
    picks = [
        sum(m * named[m] * (rank[m] == j).astype(jnp.int32) for m in range(HALF))
        for j in range(crossing)
    ]
    _, rank, _ = ranks(mine, 1 - half)
    arrived = [
        sum((p == (1 - half) * HALF + m).astype(jnp.int32) * rank[m] for m in range(HALF))
        for p in mine
    ]
    is_near = [p // HALF == half for p in mine]

    def piece(ref, c, which):
        cut = c % CUTS
        start = which * part + jnp.where(lat == 0, CUTS - 1 - cut, cut) * piece_rows
        return ref.at[c // CUTS, pl.ds(pl.multiple_of(start, HALO), piece_rows)]

    def remote(src, dst, send, recv, target):
        return pltpu.make_async_remote_copy(
            src_ref=src, dst_ref=dst, send_sem=send, recv_sem=recv,
            device_id=target, device_id_type=MESH,
        )

    def slot(local_index):
        return {"mem": half * HALF + local_index}

    def to_inner(c, to, origin):
        return remote(
            piece(block, c, to), near[c].at[origin],
            a_send.at[c, to], a_recv.at[c, origin], slot(inner_at + to),
        )

    def keep(c):
        return pltpu.make_async_copy(piece(block, c, side), near[c].at[own], a_recv.at[c, own])

    def over(c):
        return remote(sent_b.at[c], far[c], b_send.at[c], b_recv.at[c], {"mem": across})

    def to_relay(c):
        return remote(
            sent_c.at[c, 0], relayed.at[c], c_send.at[c, 0], r_recv.at[c], slot(outer_at + side)
        )

    def relay(c, origin):
        return remote(
            relayed.at[c], piece(out, c, origin),
            c_send.at[c, 0], c_recv.at[c, origin], slot(outer_at + 1 - side),
        )

    def to_outer(c, origin):
        return remote(
            sent_c.at[c, 1], piece(out, c, origin),
            c_send.at[c, 1], c_recv.at[c, origin], slot(outer_at + side),
        )

    def to_other(c, origin):
        return remote(
            sent_c.at[c, 2], piece(out, c, origin),
            c_send.at[c, 2], c_recv.at[c, origin], slot(inner_at + 1 - side),
        )

    def stay(c):
        return pltpu.make_async_copy(sent_c.at[c, 3], piece(out, c, side), c_recv.at[c, side])

    barrier = pltpu.get_barrier_semaphore()
    for step in range(1, HALF):
        pl.semaphore_signal(
            barrier, inc=1, device_id=slot((own + step) % HALF), device_id_type=MESH
        )
    pl.semaphore_signal(barrier, inc=1, device_id={"mem": across}, device_id_type=MESH)
    pl.semaphore_signal(barrier, inc=1, device_id={"lat": 1 - lat}, device_id_type=MESH)
    pl.semaphore_wait(barrier, HALF + 1)

    def targets(is_inner):
        return (1 - side,) if is_inner else (side, 1 - side)

    def send(c, is_inner):
        if c < pieces:
            for to in targets(is_inner):
                to_inner(c, to, own).start()

    def sent(c, is_inner):
        for to in targets(is_inner):
            to_inner(c, to, own).wait_send()

    for is_inner, here in ((True, inner), (False, outer)):
        @pl.when(here)
        def _():
            for c in range(pieces if is_inner else AHEAD):
                send(c, is_inner)

    @pl.when(inner)
    def _():
        for c in range(pieces):
            keep(c).start()

    def edge_copy(i, at_lat):
        first = band_rows - HALO if at_lat == 0 else 0
        src, place = ((table, fields_count), (out, 0))[i]
        return remote(
            src.at[:, pl.ds(first, HALO)], edge.at[pl.ds(place, src.shape[0])],
            e_send.at[i], e_recv.at[i], {"lat": 1 - lat},
        )

    def start_edge(i):
        for at_lat in range(2):
            @pl.when(lat == at_lat)
            def _():
                edge_copy(i, at_lat).start()

    start_edge(0)

    def pass_over(c):
        for origin in range(HALF):
            @pl.when(own == origin)
            def _():
                keep(c).wait()

            @pl.when(own != origin)
            def _():
                to_inner(c, 0, origin).wait_recv()
        for j in range(crossing):
            sent_b[c, j] = near[c][picks[j]]
        over(c).start()

    def parent_of(c, local_index):
        def pick(values):
            return sum(
                values[s] * (local_index == s).astype(jnp.int32) for s in range(HALF)
            )

        from_near = near[c][pick([p % HALF for p in mine])]
        from_far = far[c][pick(arrived)]
        return jnp.where(pick([n.astype(jnp.int32) for n in is_near]) == 1, from_near, from_far)

    def hand_out(c):
        over(c).wait_recv()
        sent_c[c, 0] = parent_of(c, outer_at + 1 - side)
        to_relay(c).start()
        sent_c[c, 1] = parent_of(c, outer_at + side)
        to_outer(c, side).start()
        sent_c[c, 2] = parent_of(c, inner_at + 1 - side)
        to_other(c, side).start()
        sent_c[c, 3] = parent_of(c, own)
        stay(c).start()

    @pl.when(inner)
    def _():
        for c in range(pieces + LAG):
            if c < pieces:
                pass_over(c)
            if c >= LAG:
                hand_out(c - LAG)

    @pl.when(outer)
    def _():
        for c in range(pieces + RELAY_LAG):
            if c < pieces:
                sent(c, False)
                send(c + AHEAD, False)
            if c >= RELAY_LAG:
                to_relay(c - RELAY_LAG).wait_recv()
                relay(c - RELAY_LAG, side).start()

    def finish(c):
        @pl.when(inner)
        def _():
            stay(c).wait()
            to_other(c, 1 - side).wait_recv()

        @pl.when(outer)
        def _():
            to_outer(c, side).wait_recv()
            relay(c, 1 - side).wait_recv()

    for c in range(pieces - 1):
        finish(c)
    start_edge(1)
    finish(pieces - 1)

    @pl.when(inner)
    def _():
        for c in range(pieces):
            sent(c, True)
            over(c).wait_send()
            to_relay(c).wait_send()
            to_outer(c, side).wait_send()
            to_other(c, side).wait_send()

    @pl.when(outer)
    def _():
        for c in range(pieces):
            relay(c, side).wait_send()

    for at_lat in range(2):
        @pl.when(lat == at_lat)
        def _():
            for i in range(2):
                edge_copy(i, at_lat).wait_send()
                edge_copy(i, 1 - at_lat).wait_recv()


def gather_parents(crossing, ancestors, block, table):
    fields_count, band_rows, columns = block.shape
    pieces = fields_count * CUTS
    part = (band_rows // PAIR // CUTS, columns)
    edge = jax.ShapeDtypeStruct((fields_count + table.shape[0], HALO, columns), jnp.float32)
    return pl.pallas_call(
        functools.partial(gather_kernel, crossing),
        out_shape=[jax.ShapeDtypeStruct(block.shape, jnp.float32), edge],
        in_specs=[pl.BlockSpec(memory_space=pltpu.SMEM)] + [pl.BlockSpec(memory_space=pl.ANY)] * 2,
        out_specs=[pl.BlockSpec(memory_space=pl.ANY)] * 2,
        scratch_shapes=[
            *[pltpu.VMEM((HALF, *part), jnp.float32)] * pieces,
            *[pltpu.VMEM((crossing, *part), jnp.float32)] * pieces,
            pltpu.VMEM((pieces, crossing, *part), jnp.float32),
            pltpu.VMEM((pieces, HALF, *part), jnp.float32),
            pltpu.VMEM((pieces, *part), jnp.float32),
            pltpu.SemaphoreType.DMA((pieces, PAIR)),
            pltpu.SemaphoreType.DMA((pieces, HALF)),
            pltpu.SemaphoreType.DMA((pieces,)),
            pltpu.SemaphoreType.DMA((pieces,)),
            pltpu.SemaphoreType.DMA((pieces, HALF)),
            pltpu.SemaphoreType.DMA((pieces, PAIR)),
            pltpu.SemaphoreType.DMA((pieces,)),
            pltpu.SemaphoreType.DMA((2,)),
            pltpu.SemaphoreType.DMA((2,)),
        ],
        compiler_params=pltpu.CompilerParams(
            collective_id=crossing, has_side_effects=True, vmem_limit_bytes=24 * 1024 * 1024
        ),
        name="gather_parents",
    )(ancestors, block, table)


def gather_by_halves(block, table, ancestors):
    groups = lax.axis_size("groups")
    lists = [ancestors] + [
        lax.ppermute(ancestors, "groups", [(i, (i + step) % groups) for i in range(groups)])
        for step in range(1, groups)
    ]
    most = pl.pallas_call(
        functools.partial(other_half_count, groups),
        out_shape=jax.ShapeDtypeStruct((1,), jnp.int32),
        in_specs=[pl.BlockSpec(memory_space=pltpu.SMEM)] * groups,
        out_specs=pl.BlockSpec(memory_space=pltpu.SMEM),
        name="other_half_count",
    )(*lists)[0]
    least = HALF // 2

    def run(crossing):
        return lambda: gather_parents(crossing, ancestors, block, table)

    return lax.switch(
        jnp.maximum(most - least, 0), [run(crossing) for crossing in range(least, HALF + 1)]
    )


def copy_members(block, ancestors):
    pieces = lax.all_to_all(block, "mem", split_axis=2, concat_axis=0, tiled=True)
    taken = jnp.take(pieces, ancestors, axis=0)
    return lax.all_to_all(taken, "mem", split_axis=0, concat_axis=2, tiled=True)[0]


def edge_rows(values):
    count = lax.axis_size("lat")
    forward = [(i, i + 1) for i in range(count - 1)]
    backward = [(target, source) for source, target in forward]
    low = lax.ppermute(values[:, -HALO:], "lat", forward)
    high = lax.ppermute(values[:, :HALO], "lat", backward)
    return low, high


def on_device(ensemble, forcing_table, ancestors, selector):
    by_halves = lax.axis_size("mem") == 2 * HALF and lax.axis_size("lat") == 2
    if by_halves and ensemble.shape[2] % (PAIR * CUTS * HALO) == 0:
        parents, edge = gather_by_halves(ensemble[0], forcing_table, ancestors)
        low, high = edge, edge
    else:
        parents = copy_members(ensemble, ancestors)
        ends = [
            jnp.concatenate([values[:, :HALO], values[:, -HALO:]], axis=1)
            for values in (parents, forcing_table)
        ]
        low, high = edge_rows(jnp.concatenate(ends, axis=0))
    return run_window(parents, low, high, forcing_table, selector, lax.axis_size("lat"))[None]


def solution(mesh):
    placed = (
        P(("groups", "mem"), None, "lat", None),
        P(None, "lat", None),
        P("groups"),
        P(("groups", "mem")),
    )
    return jax.shard_map(
        on_device,
        mesh=mesh,
        in_specs=placed,
        out_specs=P(("groups", "mem"), None, "lat", None),
        check_vma=False,
    )
```
